32 devices in a mesh: dp: 4 (over z), task: 4 (over y, core), mp: 2 (over x).
Axes of the slice: x: 2, y: 2, z: 4, core: 2. Of those that a mesh axis runs over, the one named last changes fastest.
Arguments:
- tokens: bfloat16 [3072, 2048], P(('dp', 'task')), may hold values from -6 to 6
- expert_ids: int32 [3072, 2], P(('dp', 'task')), may hold values from 0 to 3, all different within a row; in each aligned block of 192 rows (0 to 191, 192 to 383, ...) at most 120 rows name the same one
- gate_levels: int32 [3072, 2], P(('dp', 'task')), may hold values from 1 to 15
- expert_weight: bfloat16 [4, 2048, 4096], P('dp', None, 'mp'), may hold values from -0.125 to 0.125
- tower_weight: bfloat16 [4, 4096, 256], P(None, 'mp'), may hold values from -0.09375 to 0.09375
- tower_out: float32 [4, 256], P('task'), may hold values from -1.5 to 1.5
- cotangent: float32 [4, 3072], P('task', 'dp'), may hold values from -24 to 24
Outputs:
- predictions: float32 [4, 3072], P('task', 'dp')
- mix_grad: bfloat16 [3072, 4096], P(('dp', 'task'), 'mp')
The draws below stay inside these ranges and needn't reach their ends.
Inputs may be any that keep to these rules, and one draw needn't show every extreme that they name: `expert_ids`: each row names 2 different experts; in each aligned block of 192 rows (the rows of one device) no expert is named by more than 120 rows, and some expert reaches 120 in some block.
All inputs are finite; a program needn't handle non-finite values.
Results may differ from the reference program's by a relative error of at most 0.02.
Values may be sent and summed in bfloat16 or wider, within the bound.
A program may use at most 64 MiB of HBM per device.

```python
import math
import jax
import jax.numpy as jnp
import numpy as np
from jax import lax

D = 2048
H = 4096
FT = 256
TOK_DEV = 192
TOP = 2
EXPERTS = 4
TASKS = 4
CAP = 120
TOKENS = 3072


def plant(array, rng, smallest, top_value):
    longest = array.shape.index(max(array.shape))
    spots = []
    for shift in (0, 1):
        where = [jax.random.randint(jax.random.fold_in(rng, axis), (), 0, length) for axis, length in enumerate(array.shape)]
        where[longest] = (where[longest] + shift) % array.shape[longest]
        spots.append(tuple(where))
    return array.at[spots[0]].set(smallest).at[spots[1]].set(top_value)


def shard_levels(own_key, dims, pieces, low, top_value):
    def one(dim, parts):
        steps = jax.random.uniform(jax.random.fold_in(jax.random.fold_in(own_key, 6), dim), (parts,), jnp.float32, low / len(pieces), top_value / len(pieces))
        return jnp.repeat(jnp.exp(steps), dims[dim] // parts).reshape((-1,) + (1,) * (len(dims) - dim - 1))

    loudness = one(*pieces[0])
    for cut in pieces[1:]:
        loudness = loudness * one(*cut)
    return loudness


def deal_out(stream_key, own, number, rows, count, top, bound, slope):
    order = jax.random.permutation(stream_key, count)
    packed, usual = load_shares(count, rows * top, bound, slope, True), load_shares(count, rows * top, bound, slope, False)
    places = jnp.arange(count)

    def named(sizes, turn):
        used = int((sizes > 0).sum())
        fixed = max(1, used // 4)
        moved = fixed + (places - fixed + turn * (used - fixed)) % max(1, count - fixed)
        return jnp.zeros((count,), jnp.int32).at[order[jnp.where(places < fixed, places, moved)]].set(jnp.asarray(sizes, jnp.int32))

    sizes = jnp.where(number % 4 == 0, named(packed, number // 4), named(usual, number - number // 4 - 1))
    mixed = jax.random.permutation(jax.random.fold_in(own, 3), count)
    source_of, sink = mixed[0:count // 2 * 2:2], mixed[1:count // 2 * 2:2]
    margin = jnp.minimum(sizes[source_of] - 1, bound - sizes[sink]) // 2
    margin = jnp.where((source_of == order[0]) | (sink == order[0]) | (sizes[sink] == 0), 0, jnp.maximum(margin, 0))
    moved = jax.random.randint(jax.random.fold_in(own, 4), (count // 2,), 0, 1 << 20) % (margin + 1)
    sizes = sizes.at[source_of].add(-moved).at[sink].add(moved)
    items = jnp.searchsorted(jnp.cumsum(sizes), jnp.arange(rows * top), side="right").astype(jnp.int32)
    grid = items.reshape(top, rows).T
    grid = grid[jax.random.permutation(jax.random.fold_in(own, 1), rows)]
    turn = jax.random.randint(jax.random.fold_in(own, 2), (rows, 1), 0, top)
    return jnp.take_along_axis(grid, (jnp.arange(top)[None, :] + turn) % top, axis=1)


def load_shares(amount, total, limit, skew, full):
    weights = [(1 << 20) // math.isqrt(rank ** skew) + 1 for rank in range(1, amount + 1)]
    largest = limit if full else min(limit, max(-(-total // amount), total * weights[0] // sum(weights)))
    least = 1 if total - largest >= amount - 1 else 0
    holding, spare = [largest] + [least] * (amount - 1), total - largest - least * (amount - 1)
    while spare > 0:
        free = [i for i in range(1, amount) if holding[i] < largest] or [i for i in range(1, amount) if holding[i] < limit]
        mass, remaining = sum([weights[i] for i in free]), spare
        for i in free:
            extra = min(limit - holding[i], max(1, remaining * weights[i] // mass), spare)
            holding[i] = holding[i] + extra
            spare = spare - extra
    return np.array(holding)


def scatter_about(own_key, extent, spread, limit, shards=(), held_as=jnp.bfloat16):
    drawn = jax.random.normal(own_key, extent, jnp.float32) * spread
    if len(shards) > 0:
        drawn = shard_levels(own_key, extent, shards, -0.22, 0.18) * drawn
    return jnp.clip(drawn, min=-limit, max=limit).astype(held_as)


def setup_inputs(seed: int = 0) -> dict:
    streams_of = jax.random.split(jax.random.key(seed), 8)
    tokens = scatter_about(streams_of[0], (TOKENS, D), 1.0, 6.0, ((0, 16),))
    expert_ids_keys = jax.random.split(jax.random.fold_in(streams_of[1], 1), TOKENS // TOK_DEV)
    expert_ids_turns = jax.random.permutation(jax.random.fold_in(streams_of[1], 3), TOKENS // TOK_DEV)
    expert_ids = jax.vmap(lambda own, number: deal_out(jax.random.fold_in(streams_of[1], 2), own, number, TOK_DEV, EXPERTS, TOP, CAP, 2))(expert_ids_keys, expert_ids_turns).reshape((TOKENS, TOP))
    gate_levels = plant(jax.random.randint(streams_of[2], (TOKENS, TOP), 1, 16), jax.random.fold_in(streams_of[2], 1), 1, 15).astype(jnp.int32)
    expert_weight = scatter_about(streams_of[3], (EXPERTS, D, H), D ** -0.5, 0.125, ((0, 4), (2, 2)))
    tower_weight = scatter_about(streams_of[4], (TASKS, H, FT), H ** -0.5, 0.09375, ((1, 2),))
    tower_out = scatter_about(streams_of[5], (TASKS, FT), 0.25, 1.5, ((0, 4),), jnp.float32)
    cotangent = scatter_about(streams_of[6], (TASKS, TOKENS), 4.0, 24.0, ((0, 4), (1, 4)), jnp.float32)
    return {"tokens": tokens, "expert_ids": expert_ids, "gate_levels": gate_levels, "expert_weight": expert_weight, "tower_weight": tower_weight, "tower_out": tower_out, "cotangent": cotangent}


def slot_table(expert_ids):
    blocks = TOKENS // TOK_DEV
    per_block = TOK_DEV * TOP
    ids = expert_ids.reshape(blocks, per_block).astype(jnp.int32)
    onehot = (ids[:, :, None] == jnp.arange(EXPERTS, dtype=jnp.int32)[None, None, :]).astype(jnp.int32)
    rank = jnp.cumsum(onehot, axis=1) - 1
    position = jnp.sum(onehot * rank, axis=2)
    block_ids = jnp.arange(blocks, dtype=jnp.int32)[:, None]
    dest = (ids * blocks + block_ids) * CAP + position
    route_ids = jnp.arange(blocks * per_block, dtype=jnp.int32).reshape(blocks, per_block)
    table = jnp.full((EXPERTS * blocks * CAP,), TOKENS * TOP, jnp.int32)
    return table.at[dest.reshape(-1)].set(route_ids.reshape(-1))


def reference(tokens, expert_ids, gate_levels, expert_weight, tower_weight, tower_out, cotangent):
    levels = gate_levels.astype(jnp.float32)
    gates = (levels / jnp.sum(levels, axis=1, keepdims=True)).reshape(-1)
    table = slot_table(expert_ids)
    slots = (TOKENS // TOK_DEV) * CAP

    def one_expert(acc, expert):
        routes = lax.dynamic_slice_in_dim(table, (expert * slots).astype(jnp.int32), slots)
        valid = routes < TOKENS * TOP
        safe_route = jnp.where(valid, routes, 0)
        owner = safe_route // TOP
        rows = tokens[owner]
        weight = lax.dynamic_index_in_dim(expert_weight, expert, 0, keepdims=False)
        hidden = jax.nn.silu(jnp.dot(rows, weight, preferred_element_type=jnp.float32)).astype(jnp.bfloat16)
        scale = jnp.where(valid, gates[safe_route], jnp.float32(0.0))
        target = jnp.where(valid, owner, TOKENS)
        acc = acc.at[target].add(scale[:, None] * hidden.astype(jnp.float32), mode="drop")
        return acc, None

    mix_acc, unused = lax.scan(one_expert, jnp.zeros((TOKENS, H), jnp.float32), jnp.arange(EXPERTS, dtype=jnp.int32))
    mix = mix_acc.astype(jnp.bfloat16)

    def one_tower(acc, inputs):
        weight, out_vec, cot = inputs
        z = jnp.dot(mix, weight, preferred_element_type=jnp.float32)
        sig = jax.nn.sigmoid(z)
        pred = jnp.dot(z * sig, out_vec, preferred_element_type=jnp.float32)
        dz = (cot[:, None] * out_vec[None, :] * sig * (1.0 + z * (1.0 - sig))).astype(jnp.bfloat16)
        term = jnp.dot(dz, weight.T, preferred_element_type=jnp.float32).astype(jnp.bfloat16)
        term = lax.optimization_barrier(term)
        return acc + term.astype(jnp.float32), pred

    grad_acc, predictions = lax.scan(one_tower, jnp.zeros((TOKENS, H), jnp.float32), (tower_weight, tower_out, cotangent))
    return predictions, grad_acc.astype(jnp.bfloat16)
```

```python
import functools

import jax
import jax.numpy as jnp
from jax import lax
from jax.experimental import pallas as pl
from jax.experimental.pallas import tpu as pltpu
from jax.sharding import PartitionSpec as P

MESH = pl.DeviceIdType.MESH
F32 = jnp.float32
BF16 = jnp.bfloat16


def sigmoid(v):
    return 0.5 + 0.5 * jnp.tanh(0.5 * v)


def kernel(
    n, nt, m,
    tokens, ids, levels, weight, towers, tower_out, cotangent,
    pred_out, grad_out,
    tok, w, tw, disp, held, gate, hid, part, rs_out, rs_in, back_out, back_in,
    zsum, dz, small_out, small_in, pred_send, pred_in,
    load_sem, z_send, z_recv, x_send, x_recv, rs_send, rs_recv, b_send, b_recv,
    s_send, s_recv, d_send, d_recv, p_send, p_recv,
):
    zi, ti, xi = lax.axis_index("dp"), lax.axis_index("task"), lax.axis_index("mp")
    rows = ids.shape[0]
    slots = gate.shape[2]
    depth = tok.shape[2]
    units = w.shape[1]
    ft = towers.shape[2]
    tl = nt // m
    ucols = tl * ft

    def partner(o):
        other, bit = 0, 1
        while bit < n:
            other = other + bit * ((zi // bit + o // bit) % 2)
            bit *= 2
        return other

    tok_loads = []
    for j in range(m):
        tok_loads.append(pltpu.make_async_copy(
            tokens.at[:, pl.ds(j * depth, depth)], tok.at[j], load_sem.at[2 + j]))
        tok_loads[j].start()
    w_load = pltpu.make_async_copy(weight.at[0], w, load_sem.at[0])
    tw_load = pltpu.make_async_copy(towers, tw, load_sem.at[1])
    w_load.start()
    tw_load.start()

    barrier = pltpu.get_barrier_semaphore()

    def greet_line(o, c):
        pl.semaphore_signal(barrier, inc=1, device_id={"dp": partner(o)}, device_id_type=MESH)
        return c

    def greet_plane(o, c):
        at = (ti * m + xi + o) % (nt * m)
        pl.semaphore_signal(
            barrier, inc=1, device_id={"task": at // m, "mp": at % m}, device_id_type=MESH)
        return c

    lax.fori_loop(1, n, greet_line, 0)
    lax.fori_loop(1, nt * m, greet_plane, 0)

    lane = lax.broadcasted_iota(jnp.int32, (rows, 128), 1)
    first, second = ids[:, 0:1] == lane, ids[:, 1:2] == lane
    level_of = (jnp.where(first, levels[:, 0:1], 0) + jnp.where(second, levels[:, 1:2], 0)).astype(F32)
    named = jnp.where(level_of > 0, 1.0, 0.0)
    above = jnp.where(
        lax.broadcasted_iota(jnp.int32, (rows, rows), 0)
        > lax.broadcasted_iota(jnp.int32, (rows, rows), 1), 1.0, 0.0)
    rank = jnp.dot(above.astype(BF16), named.astype(BF16), preferred_element_type=F32)
    place = jnp.where(named > 0, rank, -1.0)
    scale = 1.0 / jnp.sum(level_of, axis=1, keepdims=True)
    slot = lax.broadcasted_iota(jnp.int32, (rows, slots), 1).astype(F32)

    def pick(d):
        chosen = lane == d
        here = jnp.sum(jnp.where(chosen, place, 0.0), axis=1, keepdims=True)
        level = jnp.sum(jnp.where(chosen, level_of, 0.0), axis=1, keepdims=True)
        hit = slot == here
        gate[d] = jnp.where(hit, level, 0.0).astype(BF16)
        return jnp.where(hit, 1.0, 0.0).astype(BF16)

    def gathered(spot, j):
        return lax.dot_general(
            spot, tok[j], (((0,), (0,)), ((), ())), preferred_element_type=F32).astype(BF16)

    for j in range(m):
        tok_loads[j].wait()
    pl.semaphore_wait(barrier, n - 1 + nt * m - 1)

    def dispatch_copy(o):
        d = partner(o)
        return pltpu.make_async_remote_copy(
            src_ref=disp.at[d], dst_ref=held.at[zi, xi], send_sem=z_send.at[d],
            recv_sem=z_recv.at[zi], device_id={"dp": d}, device_id_type=MESH)

    def dispatch(i, c):
        o = n - 1 - i
        d = partner(o)
        disp[d] = gathered(pick(d), xi)
        dispatch_copy(o).start()
        return c

    lax.fori_loop(0, n - 1, dispatch, 0)

    for k in range(nt):
        small_out[k, 0:1, 0:rows] = cotangent[0:1, k * rows:(k + 1) * rows]
        small_out[k, 1:2, 0:ft] = tower_out[0:1, :]

    def small_copy(o, arriving=False):
        k = (ti + o) % nt
        return pltpu.make_async_remote_copy(
            src_ref=small_out.at[k], dst_ref=small_in.at[k if arriving else ti],
            send_sem=s_send.at[k], recv_sem=s_recv.at[k if arriving else ti],
            device_id={"task": k}, device_id_type=MESH)

    def send_small(o, c):
        small_copy(o).start()
        return c

    lax.fori_loop(1, nt, send_small, 0)
    small_in[ti] = small_out[ti]

    own = pick(zi)
    for j in range(m):
        held[zi, j] = gathered(own, j)
    zsum[...] = jnp.zeros_like(zsum)
    w_load.wait()
    tw_load.wait()

    def rs_copy(s, o, arriving=False):
        j = (xi + o) % m
        return pltpu.make_async_remote_copy(
            src_ref=rs_out.at[s, j], dst_ref=rs_in.at[s, j if arriving else xi],
            send_sem=rs_send.at[s, j], recv_sem=rs_recv.at[s, j if arriving else xi],
            device_id={"mp": j}, device_id_type=MESH)

    def expert(s):
        step = 512 if units % 512 == 0 else units
        for c0 in range(0, units, step):
            acc = jnp.zeros((slots, step), F32)
            for j in range(m):
                acc += jnp.dot(
                    held[s, j], w[j * depth:(j + 1) * depth, c0:c0 + step],
                    preferred_element_type=F32)
            hid[:, c0:c0 + step] = (acc * sigmoid(acc)).astype(BF16)
        for t in range(nt):
            u = jnp.dot(hid[...], tw[t], preferred_element_type=F32)
            c0 = (t % tl) * ft
            rs_out[s, t // tl, :, c0:c0 + ft] = u.astype(BF16)
        for o in range(1, m):
            rs_copy(s, o).start()

    def reduced(s):
        total = rs_out[s, xi].astype(F32)
        for o in range(1, m):
            rs_copy(s, o, True).wait_recv()
            total += rs_in[s, (xi + o) % m].astype(F32)
        return total.astype(BF16)

    def back_copy(s, arriving=False):
        return pltpu.make_async_remote_copy(
            src_ref=back_out.at[s], dst_ref=back_in.at[s if arriving else zi],
            send_sem=b_send.at[s], recv_sem=b_recv.at[s if arriving else zi],
            device_id={"dp": s}, device_id_type=MESH)

    def forward_copy(s, o, arriving=False):
        j = (xi + o) % m
        at = j if arriving else xi
        return pltpu.make_async_remote_copy(
            src_ref=held.at[s, at], dst_ref=held.at[s, at],
            send_sem=x_send.at[s, j], recv_sem=x_recv.at[s, at],
            device_id={"mp": j}, device_id_type=MESH)

    def arrive(s):
        pltpu.make_async_remote_copy(
            src_ref=disp.at[s], dst_ref=held.at[s, xi], send_sem=z_send.at[s],
            recv_sem=z_recv.at[s], device_id={"dp": s}, device_id_type=MESH).wait_recv()
        for o in range(1, m):
            forward_copy(s, o).start()

    def send_back(s):
        back_out[s] = reduced(s)
        back_copy(s).start()

    expert(zi)

    def work(o, c):
        s = partner(o)
        arrive(s)

        @pl.when(o > 1)
        def _():
            send_back(partner(o - 1))

        for p in range(1, m):
            forward_copy(s, p, True).wait_recv()
        expert(s)
        return c

    lax.fori_loop(1, n, work, 0)
    zsum[...] += jnp.dot(gate[zi], reduced(zi), preferred_element_type=F32)
    send_back(partner(n - 1))

    def collect(o, c):
        s = partner(o)
        back_copy(s, True).wait_recv()
        zsum[...] += jnp.dot(gate[s], back_in[s], preferred_element_type=F32)
        return c

    lax.fori_loop(1, n, collect, 0)

    def small_arrive(o, c):
        small_copy(o, True).wait_recv()
        return c

    lax.fori_loop(1, nt, small_arrive, 0)

    diagonal = (
        lax.broadcasted_iota(jnp.int32, (rows, rows), 0)
        == lax.broadcasted_iota(jnp.int32, (rows, rows), 1))

    def pred_copy(l, o):
        y = (xi + o) % m
        return pltpu.make_async_remote_copy(
            src_ref=pred_send.at[l], dst_ref=pred_in.at[ti], send_sem=p_send.at[l, o],
            recv_sem=p_recv.at[ti], device_id={"task": xi * tl + l, "mp": y},
            device_id_type=MESH)

    for l in range(tl):
        t = xi * tl + l
        z = zsum[:, l * ft:(l + 1) * ft] * scale
        s = sigmoid(z)
        out_row = small_in[t, 1:2, 0:ft]
        cot = jnp.sum(jnp.where(diagonal, small_in[t, 0:1, 0:rows], 0.0), axis=1, keepdims=True)
        dz[t] = (cot * out_row * s * (1.0 + z * (1.0 - s))).astype(BF16)
        pred = jnp.sum(z * s * out_row, axis=1, keepdims=True)
        pred_send[l, 0:1, 0:rows] = jnp.sum(jnp.where(diagonal, pred, 0.0), axis=0, keepdims=True)

    def dz_copy(o, arriving=False):
        j = (xi + o) % m
        at = pl.ds((j if arriving else xi) * tl, tl)
        return pltpu.make_async_remote_copy(
            src_ref=dz.at[at], dst_ref=dz.at[at], send_sem=d_send.at[j],
            recv_sem=d_recv.at[j if arriving else xi], device_id={"mp": j}, device_id_type=MESH)

    for o in range(1, m):
        dz_copy(o).start()
    for l in range(tl):
        mine = ti == xi * tl + l

        @pl.when(mine)
        def _():
            pred_in[ti] = pred_send[l]

        @pl.when(jnp.logical_not(mine))
        def _():
            pred_copy(l, 0).start()

        for o in range(1, m):
            pred_copy(l, o).start()

    for o in range(1, m):
        dz_copy(o, True).wait_recv()
    step = 512 if units % 512 == 0 else units
    for c0 in range(0, units, step):
        acc = jnp.zeros((rows, step), F32)
        for t in range(nt):
            acc += lax.dot_general(
                dz[t], tw[t, c0:c0 + step, :], (((1,), (1,)), ((), ())),
                preferred_element_type=F32)
        grad_out[:, c0:c0 + step] = acc.astype(BF16)

    keeper = ti // tl
    for k in range(nt):
        @pl.when(jnp.logical_not(jnp.logical_and(keeper == xi, ti == k)))
        def _():
            pltpu.make_async_remote_copy(
                src_ref=pred_send.at[0], dst_ref=pred_in.at[k], send_sem=p_send.at[0, 0],
                recv_sem=p_recv.at[k], device_id={"task": (ti + 1) % nt},
                device_id_type=MESH).wait_recv()

        pred_out[0:1, k * rows:(k + 1) * rows] = pred_in[k, 0:1, 0:rows]

    def drain(o, c):
        s = partner(o)
        dispatch_copy(o).wait_send()
        back_copy(s).wait_send()
        for p in range(1, m):
            forward_copy(s, p).wait_send()
            rs_copy(s, p).wait_send()
        return c

    lax.fori_loop(1, n, drain, 0)
    for p in range(1, m):
        rs_copy(zi, p).wait_send()
        dz_copy(p).wait_send()

    def drain_small(o, c):
        small_copy(o).wait_send()
        return c

    lax.fori_loop(1, nt, drain_small, 0)
    for l in range(tl):
        @pl.when(ti != xi * tl + l)
        def _():
            pred_copy(l, 0).wait_send()

        for o in range(1, m):
            pred_copy(l, o).wait_send()


def body(tokens, expert_ids, gate_levels, expert_weight, tower_weight, tower_out, cotangent):
    n, nt, m = lax.axis_size("dp"), lax.axis_size("task"), lax.axis_size("mp")
    rows, top = expert_ids.shape
    width, units = expert_weight.shape[1:]
    ft = tower_weight.shape[2]
    slots = -(-(5 * rows * top // (4 * n)) // 16) * 16
    depth = width // m
    tl = nt // m
    ucols = tl * ft
    wide = -(-max(rows, ft) // 128) * 128
    vmem = pl.BlockSpec(memory_space=pltpu.VMEM)
    hbm = pl.BlockSpec(memory_space=pl.ANY)
    dma = pltpu.SemaphoreType.DMA
    return tuple(pl.pallas_call(
        functools.partial(kernel, n, nt, m),
        out_shape=(
            jax.ShapeDtypeStruct((1, nt * rows), F32),
            jax.ShapeDtypeStruct((rows, units), BF16),
        ),
        in_specs=[hbm, vmem, vmem, hbm, hbm, vmem, vmem],
        out_specs=(vmem, vmem),
        scratch_shapes=[
            pltpu.VMEM((m, rows, depth), BF16),
            pltpu.VMEM((width, units), BF16),
            pltpu.VMEM(tower_weight.shape, BF16),
            pltpu.VMEM((n, slots, depth), BF16),
            pltpu.VMEM((n, m, slots, depth), BF16),
            pltpu.VMEM((n, rows, slots), BF16),
            pltpu.VMEM((slots, units), BF16),
            pltpu.VMEM((8, 128), F32),
            pltpu.VMEM((n, m, slots, ucols), BF16),
            pltpu.VMEM((n, m, slots, ucols), BF16),
            pltpu.VMEM((n, slots, ucols), BF16),
            pltpu.VMEM((n, slots, ucols), BF16),
            pltpu.VMEM((rows, ucols), F32),
            pltpu.VMEM((nt, rows, ft), BF16),
            pltpu.VMEM((nt, 8, wide), F32),
            pltpu.VMEM((nt, 8, wide), F32),
            pltpu.VMEM((tl, 8, wide), F32),
            pltpu.VMEM((nt, 8, wide), F32),
            dma((2 + m,)),
            dma((n,)), dma((n,)),
            dma((n, m)), dma((n, m)),
            dma((n, m)), dma((n, m)),
            dma((n,)), dma((n,)),
            dma((nt,)), dma((nt,)),
            dma((m,)), dma((m,)),
            dma((tl, m)), dma((nt,)),
        ],
        compiler_params=pltpu.CompilerParams(
            collective_id=0, has_side_effects=True, vmem_limit_bytes=48 * 1024 * 1024),
        name="expert_towers",
    )(tokens, expert_ids, gate_levels, expert_weight, tower_weight, tower_out, cotangent))


def solution(mesh):
    return jax.shard_map(
        body,
        mesh=mesh,
        in_specs=(
            P(("dp", "task"), None),
            P(("dp", "task"), None),
            P(("dp", "task"), None),
            P("dp", None, "mp"),
            P(None, "mp", None),
            P("task", None),
            P("task", "dp"),
        ),
        out_specs=(P("task", "dp"), P(("dp", "task"), "mp")),
        check_vma=False,
    )
```

```python
import functools

import jax
import jax.numpy as jnp
from jax import lax
from jax.experimental import pallas as pl
from jax.experimental.pallas import tpu as pltpu
from jax.sharding import PartitionSpec as P

MESH = pl.DeviceIdType.MESH
F32 = jnp.float32
BF16 = jnp.bfloat16


def sigmoid(v):
    return 0.5 + 0.5 * jnp.tanh(0.5 * v)


def kernel(
    n, nt, m,
    tokens, ids_in, levels_in, weight, towers, tower_out_in, cotangent_in,
    pred_out, grad_out,
    tok, w, tw, ids, levels, tower_out, cotangent,
    disp, held, gate, pre, hid, part, rs_out, rs_in, back_out, back_in,
    zsum, dz, gsum, small_out, small_in, pred_send, pred_in,
    load_sem, z_send, z_recv, x_send, x_recv, rs_send, rs_recv, b_send, b_recv,
    s_send, s_recv, d_send, d_recv, p_send, p_recv,
):
    zi, ti, xi = lax.axis_index("dp"), lax.axis_index("task"), lax.axis_index("mp")
    rows = ids.shape[1]
    slots = gate.shape[2]
    chunks, _, depth = tok.shape
    each = chunks // m
    units = w.shape[1]
    ft = towers.shape[2]
    tl = nt // m
    step = 512 if units % 512 == 0 else units

    def partner(o):
        other, bit = 0, 1
        while bit < n:
            other = other + bit * ((zi // bit + o // bit) % 2)
            bit *= 2
        return other

    def load(src, dst, i):
        copy = pltpu.make_async_copy(src, dst, load_sem.at[i])
        copy.start()
        return copy

    routing = [load(ids_in, ids, 0), load(levels_in, levels, 1)]
    tok_loads = [
        load(tokens.at[:, pl.ds(c * depth, depth)], tok.at[c], 6 + c) for c in range(chunks)]
    small_loads = [load(tower_out_in, tower_out, 2), load(cotangent_in, cotangent, 3)]
    w_load = load(weight.at[0], w, 4)
    tw_load = load(towers, tw, 5)

    barrier = pltpu.get_barrier_semaphore()

    def greet_line(o, c):
        pl.semaphore_signal(barrier, inc=1, device_id={"dp": partner(o)}, device_id_type=MESH)
        return c

    def greet_plane(o, c):
        at = (ti * m + xi + o) % (nt * m)
        pl.semaphore_signal(
            barrier, inc=1, device_id={"task": at // m, "mp": at % m}, device_id_type=MESH)
        return c

    lax.fori_loop(1, n, greet_line, 0)
    lax.fori_loop(1, nt * m, greet_plane, 0)

    for copy in routing:
        copy.wait()
    names = max(8, n)
    sub = lax.broadcasted_iota(jnp.int32, (names, rows), 0)
    level_of = (
        jnp.where(ids[0:1, :] == sub, levels[0:1, :], 0)
        + jnp.where(ids[1:2, :] == sub, levels[1:2, :], 0)).astype(F32)
    named = jnp.where(level_of > 0, 1.0, 0.0)
    down = lax.broadcasted_iota(jnp.int32, (rows, rows), 0)
    across = lax.broadcasted_iota(jnp.int32, (rows, rows), 1)
    diagonal = down == across
    before = jnp.where(down < across, 1.0, 0.0)
    rank = jnp.dot(named.astype(BF16), before.astype(BF16), preferred_element_type=F32)
    place = jnp.where(named > 0, rank, -1.0)

    def row_of(table, d):
        return jnp.sum(jnp.where(sub == d, table, 0.0), axis=0, keepdims=True)

    def column(row):
        return jnp.sum(jnp.where(diagonal, row, 0.0), axis=1, keepdims=True)

    slot_down = lax.broadcasted_iota(jnp.int32, (slots, rows), 0).astype(F32)
    slot_across = lax.broadcasted_iota(jnp.int32, (rows, slots), 1).astype(F32)

    def pick(d):
        return jnp.where(slot_down == row_of(place, d), 1.0, 0.0).astype(BF16)

    def gathered(spot, c):
        return jnp.dot(spot, tok[c], preferred_element_type=F32).astype(BF16)

    for copy in tok_loads:
        copy.wait()

    def dispatch_copy(o, c, arriving=False):
        d = partner(o)
        return pltpu.make_async_remote_copy(
            src_ref=disp.at[d, c], dst_ref=held.at[d if arriving else zi, c],
            send_sem=z_send.at[d, c], recv_sem=z_recv.at[d if arriving else zi, c],
            device_id={"dp": d}, device_id_type=MESH)

    def fill(o, first, count):
        d = partner(o)
        spot = pick(d)
        for q in range(count):
            disp[d, first + q] = gathered(spot, first + q)

    fill(2, xi * each, each)
    pl.semaphore_wait(barrier, n - 1 + nt * m - 1)
    for q in range(each):
        dispatch_copy(2, xi * each + q).start()
    fill(1, 0, chunks)
    for c in range(chunks):
        dispatch_copy(1, c).start()

    def fill_rest(o, c):
        fill(o, xi * each, each)
        return c

    lax.fori_loop(3, n, fill_rest, 0)

    for copy in small_loads:
        copy.wait()
    for k in range(nt):
        small_out[k, 0:1, 0:rows] = cotangent[0:1, k * rows:(k + 1) * rows]
        small_out[k, 1:2, 0:ft] = tower_out[0:1, :]

    def small_copy(o, arriving=False):
        k = (ti + o) % nt
        return pltpu.make_async_remote_copy(
            src_ref=small_out.at[k], dst_ref=small_in.at[k if arriving else ti],
            send_sem=s_send.at[k], recv_sem=s_recv.at[k if arriving else ti],
            device_id={"task": k}, device_id_type=MESH)

    def send_small(o, c):
        small_copy(o).start()
        return c

    lax.fori_loop(1, nt, send_small, 0)
    small_in[ti] = small_out[ti]

    own = pick(zi)
    for c in range(chunks):
        held[zi, c] = gathered(own, c)

    def set_gate(d, c):
        hit = slot_across == column(row_of(place, d))
        gate[d] = jnp.where(hit, column(row_of(level_of, d)), 0.0).astype(BF16)
        return c

    lax.fori_loop(0, n, set_gate, 0)
    scale = 1.0 / column(jnp.sum(level_of, axis=0, keepdims=True))
    zsum[...] = jnp.zeros_like(zsum)
    w_load.wait()
    tw_load.wait()

    def rs_copy(s, o, arriving=False):
        j = (xi + o) % m
        return pltpu.make_async_remote_copy(
            src_ref=rs_out.at[s, j], dst_ref=rs_in.at[s, j if arriving else xi],
            send_sem=rs_send.at[s, j], recv_sem=rs_recv.at[s, j if arriving else xi],
            device_id={"mp": j}, device_id_type=MESH)

    def partial_pre(s, first, count, c0):
        acc = jnp.zeros((slots, step), F32)
        for q in range(count):
            at = first + q
            acc += jnp.dot(
                held[s, at], w[pl.ds(pl.multiple_of(at * depth, depth), depth), c0:c0 + step],
                preferred_element_type=F32)
        return acc

    def activate(acc, c0):
        hid[:, c0:c0 + step] = (acc * sigmoid(acc)).astype(BF16)

    def expert_whole(s):
        for c0 in range(0, units, step):
            activate(partial_pre(s, 0, chunks, c0), c0)

    def expert_own_columns(s):
        for c0 in range(0, units, step):
            pre[:, c0:c0 + step] = partial_pre(s, xi * each, each, c0)

    def expert_other_columns(s):
        for o in range(1, m):
            for q in range(each):
                forward_copy(s, o, q, True).wait_recv()
        for c0 in range(0, units, step):
            acc = pre[:, c0:c0 + step]
            for o in range(1, m):
                acc += partial_pre(s, (xi + o) % m * each, each, c0)
            activate(acc, c0)

    def tower_sums(s):
        for o in list(range(1, m)) + [0]:
            j = (xi + o) % m
            for l in range(tl):
                u = jnp.dot(hid[...], tw[j * tl + l], preferred_element_type=F32)
                if o == 0:
                    part[s, :, l * ft:(l + 1) * ft] = u
                else:
                    rs_out[s, j, :, l * ft:(l + 1) * ft] = u.astype(BF16)
            if o > 0:
                rs_copy(s, o).start()

    def reduced(s):
        total = part[s]
        for o in range(1, m):
            rs_copy(s, o, True).wait_recv()
            total += rs_in[s, (xi + o) % m].astype(F32)
        return total.astype(BF16)

    def back_copy(s, arriving=False):
        return pltpu.make_async_remote_copy(
            src_ref=back_out.at[s], dst_ref=back_in.at[s if arriving else zi],
            send_sem=b_send.at[s], recv_sem=b_recv.at[s if arriving else zi],
            device_id={"dp": s}, device_id_type=MESH)

    def forward_copy(s, o, q, arriving=False):
        j = (xi + o) % m
        at = (j if arriving else xi) * each + q
        return pltpu.make_async_remote_copy(
            src_ref=held.at[s, at], dst_ref=held.at[s, at],
            send_sem=x_send.at[s, j, q], recv_sem=x_recv.at[s, at],
            device_id={"mp": j}, device_id_type=MESH)

    def arrive(o):
        for q in range(each):
            dispatch_copy(o, xi * each + q, True).wait_recv()
            for p in range(1, m):
                forward_copy(partner(o), p, q).start()

    def send_back(s):
        back_out[s] = reduced(s)
        back_copy(s).start()

    expert_whole(zi)
    tower_sums(zi)

    def work(o, c):
        s = partner(o)
        for q in range(each):
            dispatch_copy(o, xi * each + q).wait_send()
            dispatch_copy(o + 1, xi * each + q).start()
        arrive(o)

        @pl.when(o > 2)
        def _():
            send_back(partner(o - 1))

        expert_own_columns(s)
        expert_other_columns(s)
        tower_sums(s)
        return c

    lax.fori_loop(2, n - 1, work, 0)
    near, last = partner(1), partner(n - 1)
    arrive(n - 1)
    send_back(partner(n - 2))
    for c in range(chunks):
        dispatch_copy(1, c, True).wait_recv()
    expert_whole(near)
    tower_sums(near)
    expert_own_columns(last)
    send_back(near)
    expert_other_columns(last)
    tower_sums(last)
    zsum[...] += jnp.dot(gate[zi], reduced(zi), preferred_element_type=F32)
    send_back(last)

    def collect(s):
        back_copy(s, True).wait_recv()
        zsum[...] += jnp.dot(gate[s], back_in[s], preferred_element_type=F32)

    def collect_step(o, c):
        collect(partner(o))
        return c

    lax.fori_loop(2, n - 1, collect_step, 0)
    collect(near)

    def small_arrive(o, c):
        small_copy(o, True).wait_recv()
        return c

    lax.fori_loop(1, nt, small_arrive, 0)
    cots = [column(small_in[xi * tl + l, 0:1, 0:rows]) for l in range(tl)]
    collect(last)

    def pred_copy(l, o):
        y = (xi + o) % m
        return pltpu.make_async_remote_copy(
            src_ref=pred_send.at[l], dst_ref=pred_in.at[ti], send_sem=p_send.at[l, o],
            recv_sem=p_recv.at[ti], device_id={"task": xi * tl + l, "mp": y},
            device_id_type=MESH)

    def dz_copy(l, o, arriving=False):
        j = (xi + o) % m
        at = (j if arriving else xi) * tl + l
        return pltpu.make_async_remote_copy(
            src_ref=dz.at[at], dst_ref=dz.at[at], send_sem=d_send.at[j, l],
            recv_sem=d_recv.at[at], device_id={"mp": j}, device_id_type=MESH)

    for l in range(tl):
        t = xi * tl + l
        z = zsum[:, l * ft:(l + 1) * ft] * scale
        s = sigmoid(z)
        out_row = small_in[t, 1:2, 0:ft]
        dz[t] = (cots[l] * out_row * s * (1.0 + z * (1.0 - s))).astype(BF16)
        for o in range(1, m):
            dz_copy(l, o).start()
        pred = jnp.sum(z * s * out_row, axis=1, keepdims=True)
        pred_send[l, 0:1, 0:rows] = jnp.sum(jnp.where(diagonal, pred, 0.0), axis=0, keepdims=True)
        mine = ti == t

        @pl.when(mine)
        def _():
            pred_in[ti] = pred_send[l]

        @pl.when(jnp.logical_not(mine))
        def _():
            pred_copy(l, 0).start()

        for o in range(1, m):
            pred_copy(l, o).start()

    def grad(o, c0):
        acc = jnp.zeros((rows, step), F32)
        for l in range(tl):
            t = (xi + o) % m * tl + l
            acc += lax.dot_general(
                dz[t], tw[t, c0:c0 + step, :], (((1,), (1,)), ((), ())),
                preferred_element_type=F32)
        return acc

    for c0 in range(0, units, step):
        gsum[:, c0:c0 + step] = grad(0, c0)
    for o in range(1, m):
        for l in range(tl):
            dz_copy(l, o, True).wait_recv()
    for c0 in range(0, units, step):
        acc = gsum[:, c0:c0 + step]
        for o in range(1, m):
            acc += grad(o, c0)
        grad_out[:, c0:c0 + step] = acc.astype(BF16)

    keeper = ti // tl
    for k in range(nt):
        @pl.when(jnp.logical_not(jnp.logical_and(keeper == xi, ti == k)))
        def _():
            pltpu.make_async_remote_copy(
                src_ref=pred_send.at[0], dst_ref=pred_in.at[k], send_sem=p_send.at[0, 0],
                recv_sem=p_recv.at[k], device_id={"task": (ti + 1) % nt},
                device_id_type=MESH).wait_recv()

        pred_out[0:1, k * rows:(k + 1) * rows] = pred_in[k, 0:1, 0:rows]

    def drain(o, c):
        s = partner(o)
        back_copy(s).wait_send()
        for p in range(1, m):
            rs_copy(s, p).wait_send()
        return c

    def drain_far(o, c):
        for p in range(1, m):
            for q in range(each):
                forward_copy(partner(o), p, q).wait_send()
        return c

    lax.fori_loop(1, n, drain, 0)
    lax.fori_loop(2, n, drain_far, 0)
    for c in range(chunks):
        dispatch_copy(1, c).wait_send()
    for q in range(each):
        dispatch_copy(n - 1, xi * each + q).wait_send()
    for p in range(1, m):
        rs_copy(zi, p).wait_send()
        for l in range(tl):
            dz_copy(l, p).wait_send()

    def drain_small(o, c):
        small_copy(o).wait_send()
        return c

    lax.fori_loop(1, nt, drain_small, 0)
    for l in range(tl):
        @pl.when(ti != xi * tl + l)
        def _():
            pred_copy(l, 0).wait_send()

        for o in range(1, m):
            pred_copy(l, o).wait_send()


def body(tokens, expert_ids, gate_levels, expert_weight, tower_weight, tower_out, cotangent):
    n, nt, m = lax.axis_size("dp"), lax.axis_size("task"), lax.axis_size("mp")
    rows, top = expert_ids.shape
    width, units = expert_weight.shape[1:]
    ft = tower_weight.shape[2]
    slots = -(-(5 * rows * top // (4 * n)) // 16) * 16
    depth = width // m
    tl = nt // m
    ucols = tl * ft
    wide = -(-max(rows, ft) // 128) * 128
    each = 2
    chunks = m * each
    depth = width // chunks
    vmem = pl.BlockSpec(memory_space=pltpu.VMEM)
    hbm = pl.BlockSpec(memory_space=pltpu.HBM)
    dma = pltpu.SemaphoreType.DMA
    return tuple(pl.pallas_call(
        functools.partial(kernel, n, nt, m),
        out_shape=(
            jax.ShapeDtypeStruct((1, nt * rows), F32),
            jax.ShapeDtypeStruct((rows, units), BF16),
        ),
        in_specs=[hbm] * 7,
        out_specs=(vmem, vmem),
        scratch_shapes=[
            pltpu.VMEM((chunks, rows, depth), BF16),
            pltpu.VMEM((width, units), BF16),
            pltpu.VMEM(tower_weight.shape, BF16),
            pltpu.VMEM((top, rows), jnp.int32),
            pltpu.VMEM((top, rows), jnp.int32),
            pltpu.VMEM(tower_out.shape, F32),
            pltpu.VMEM(cotangent.shape, F32),
            pltpu.VMEM((n, chunks, slots, depth), BF16),
            pltpu.VMEM((n, chunks, slots, depth), BF16),
            pltpu.VMEM((n, rows, slots), BF16),
            pltpu.VMEM((slots, units), F32),
            pltpu.VMEM((slots, units), BF16),
            pltpu.VMEM((n, slots, ucols), F32),
            pltpu.VMEM((n, m, slots, ucols), BF16),
            pltpu.VMEM((n, m, slots, ucols), BF16),
            pltpu.VMEM((n, slots, ucols), BF16),
            pltpu.VMEM((n, slots, ucols), BF16),
            pltpu.VMEM((rows, ucols), F32),
            pltpu.VMEM((nt, rows, ft), BF16),
            pltpu.VMEM((rows, units), F32),
            pltpu.VMEM((nt, 8, wide), F32),
            pltpu.VMEM((nt, 8, wide), F32),
            pltpu.VMEM((tl, 8, wide), F32),
            pltpu.VMEM((nt, 8, wide), F32),
            dma((6 + chunks,)),
            dma((n, chunks)), dma((n, chunks)),
            dma((n, m, each)), dma((n, chunks)),
            dma((n, m)), dma((n, m)),
            dma((n,)), dma((n,)),
            dma((nt,)), dma((nt,)),
            dma((m, tl)), dma((nt,)),
            dma((tl, m)), dma((nt,)),
        ],
        compiler_params=pltpu.CompilerParams(
            collective_id=0, has_side_effects=True, vmem_limit_bytes=40 * 1024 * 1024),
        name="expert_towers",
    )(tokens, expert_ids.T, gate_levels.T, expert_weight, tower_weight, tower_out, cotangent))


def solution(mesh):
    return jax.shard_map(
        body,
        mesh=mesh,
        in_specs=(
            P(("dp", "task"), None),
            P(("dp", "task"), None),
            P(("dp", "task"), None),
            P("dp", None, "mp"),
            P(None, "mp", None),
            P("task", None),
            P("task", "dp"),
        ),
        out_specs=(P("task", "dp"), P(("dp", "task"), "mp")),
        check_vma=False,
    )
```

```python
import functools

import jax
import jax.numpy as jnp
from jax import lax
from jax.experimental import pallas as pl
from jax.experimental.pallas import tpu as pltpu
from jax.sharding import PartitionSpec as P

MESH = pl.DeviceIdType.MESH
F32 = jnp.float32
BF16 = jnp.bfloat16


def sigmoid(v):
    return 0.5 + 0.5 * jnp.tanh(0.5 * v)


def kernel(
    n, nt, m,
    tokens, ids_in, levels_in, weight, towers, tower_out_in, cotangent_in,
    pred_out, grad_out,
    tok, w, tw, ids, levels, tower_out, cotangent,
    disp, held, gate, pre, hid, part, rs_out, rs_in, back_out, back_in,
    zsum, dz, gsum, gout, pred, small_out, small_in, pred_send, pred_in,
    load_sem, z_send, z_recv, x_send, x_recv, rs_send, rs_recv, b_send, b_recv,
    s_send, s_recv, d_send, d_recv, p_send, p_recv, out_sem,
):
    zi, ti, xi = lax.axis_index("dp"), lax.axis_index("task"), lax.axis_index("mp")
    rows = ids.shape[1]
    slots = gate.shape[2]
    chunks, _, depth = tok.shape
    each = chunks // m
    units = w.shape[1]
    ft = towers.shape[2]
    tl = nt // m
    step = 512 if units % 512 == 0 else units

    def partner(o):
        other, bit = 0, 1
        while bit < n:
            other = other + bit * ((zi // bit + o // bit) % 2)
            bit *= 2
        return other

    def load(src, dst, i):
        copy = pltpu.make_async_copy(src, dst, load_sem.at[i])
        copy.start()
        return copy

    routing = [load(ids_in, ids, 0), load(levels_in, levels, 1)]
    tok_loads = [
        load(tokens.at[:, pl.ds(c * depth, depth)], tok.at[c], 6 + c) for c in range(chunks)]
    small_loads = [load(tower_out_in, tower_out, 2), load(cotangent_in, cotangent, 3)]
    w_load = load(weight.at[0], w, 4)
    tw_load = load(towers, tw, 5)

    barrier = pltpu.get_barrier_semaphore()

    def greet_line(o, c):
        pl.semaphore_signal(barrier, inc=1, device_id={"dp": partner(o)}, device_id_type=MESH)
        return c

    def greet_plane(o, c):
        at = (ti * m + xi + o) % (nt * m)
        pl.semaphore_signal(
            barrier, inc=1, device_id={"task": at // m, "mp": at % m}, device_id_type=MESH)
        return c

    lax.fori_loop(1, n, greet_line, 0)
    lax.fori_loop(1, nt * m, greet_plane, 0)

    for copy in routing:
        copy.wait()
    names = max(8, n)
    sub = lax.broadcasted_iota(jnp.int32, (names, rows), 0)
    level_of = (
        jnp.where(ids[0:1, :] == sub, levels[0:1, :], 0)
        + jnp.where(ids[1:2, :] == sub, levels[1:2, :], 0)).astype(F32)
    named = jnp.where(level_of > 0, 1.0, 0.0)
    down = lax.broadcasted_iota(jnp.int32, (rows, rows), 0)
    across = lax.broadcasted_iota(jnp.int32, (rows, rows), 1)
    diagonal = down == across
    before = jnp.where(down < across, 1.0, 0.0)
    rank = jnp.dot(named.astype(BF16), before.astype(BF16), preferred_element_type=F32)
    place = jnp.where(named > 0, rank, -1.0)

    def row_of(table, d):
        return jnp.sum(jnp.where(sub == d, table, 0.0), axis=0, keepdims=True)

    def column(row):
        return jnp.sum(jnp.where(diagonal, row, 0.0), axis=1, keepdims=True)

    slot_down = lax.broadcasted_iota(jnp.int32, (slots, rows), 0).astype(F32)
    slot_across = lax.broadcasted_iota(jnp.int32, (rows, slots), 1).astype(F32)

    def pick(d):
        return jnp.where(slot_down == row_of(place, d), 1.0, 0.0).astype(BF16)

    def gathered(spot, c):
        return jnp.dot(spot, tok[c], preferred_element_type=F32).astype(BF16)

    for copy in tok_loads:
        copy.wait()

    def dispatch_copy(o, c, arriving=False):
        d = partner(o)
        return pltpu.make_async_remote_copy(
            src_ref=disp.at[d, c], dst_ref=held.at[d if arriving else zi, c],
            send_sem=z_send.at[d, c], recv_sem=z_recv.at[d if arriving else zi, c],
            device_id={"dp": d}, device_id_type=MESH)

    def fill(o, first, count):
        d = partner(o)
        spot = pick(d)
        for q in range(count):
            disp[d, first + q] = gathered(spot, first + q)

    fill(2, xi * each, each)
    pl.semaphore_wait(barrier, n - 1 + nt * m - 1)
    for q in range(each):
        dispatch_copy(2, xi * each + q).start()
    fill(1, 0, chunks)
    for c in range(chunks):
        dispatch_copy(1, c).start()

    def fill_rest(o, c):
        fill(o, xi * each, each)
        return c

    lax.fori_loop(3, n, fill_rest, 0)

    for copy in small_loads:
        copy.wait()
    for k in range(nt):
        small_out[k, 0:1, 0:rows] = cotangent[0:1, k * rows:(k + 1) * rows]
        small_out[k, 1:2, 0:ft] = tower_out[0:1, :]

    def small_copy(o, arriving=False):
        k = (ti + o) % nt
        return pltpu.make_async_remote_copy(
            src_ref=small_out.at[k], dst_ref=small_in.at[k if arriving else ti],
            send_sem=s_send.at[k], recv_sem=s_recv.at[k if arriving else ti],
            device_id={"task": k}, device_id_type=MESH)

    def send_small(o, c):
        small_copy(o).start()
        return c

    lax.fori_loop(1, nt, send_small, 0)
    small_in[ti] = small_out[ti]

    own = pick(zi)
    for c in range(chunks):
        held[zi, c] = gathered(own, c)

    def set_gate(d, c):
        hit = slot_across == column(row_of(place, d))
        gate[d] = jnp.where(hit, column(row_of(level_of, d)), 0.0).astype(BF16)
        return c

    lax.fori_loop(0, n, set_gate, 0)
    scale = 1.0 / column(jnp.sum(level_of, axis=0, keepdims=True))
    zsum[...] = jnp.zeros_like(zsum)
    w_load.wait()
    tw_load.wait()

    def rs_copy(s, o, l, arriving=False):
        j = (xi + o) % m
        return pltpu.make_async_remote_copy(
            src_ref=rs_out.at[s, j, l], dst_ref=rs_in.at[s, j if arriving else xi, l],
            send_sem=rs_send.at[s, j, l], recv_sem=rs_recv.at[s, j if arriving else xi, l],
            device_id={"mp": j}, device_id_type=MESH)

    def partial_pre(s, first, count, c0):
        acc = jnp.zeros((slots, step), F32)
        for q in range(count):
            at = first + q
            acc += jnp.dot(
                held[s, at], w[pl.ds(pl.multiple_of(at * depth, depth), depth), c0:c0 + step],
                preferred_element_type=F32)
        return acc

    def activate(acc, c0):
        hid[:, c0:c0 + step] = (acc * sigmoid(acc)).astype(BF16)

    def expert_whole(s):
        for c0 in range(0, units, step):
            activate(partial_pre(s, 0, chunks, c0), c0)

    def expert_own_columns(s):
        for c0 in range(0, units, step):
            pre[:, c0:c0 + step] = partial_pre(s, xi * each, each, c0)

    def expert_other_columns(s):
        for o in range(1, m):
            for q in range(each):
                forward_copy(s, o, q, True).wait_recv()
        for c0 in range(0, units, step):
            acc = pre[:, c0:c0 + step]
            for o in range(1, m):
                acc += partial_pre(s, (xi + o) % m * each, each, c0)
            activate(acc, c0)

    def tower_sums(s):
        for o in range(1, m):
            for l in range(tl):
                j = (xi + o) % m
                u = jnp.dot(hid[...], tw[j * tl + l], preferred_element_type=F32)
                rs_out[s, j, l] = u.astype(BF16)
                rs_copy(s, o, l).start()
        for l in range(tl):
            part[s, l] = jnp.dot(hid[...], tw[xi * tl + l], preferred_element_type=F32)

    def reduced(s, l):
        total = part[s, l]
        for o in range(1, m):
            rs_copy(s, o, l, True).wait_recv()
            total += rs_in[s, (xi + o) % m, l].astype(F32)
        return total.astype(BF16)

    def back_copy(s, l, arriving=False):
        return pltpu.make_async_remote_copy(
            src_ref=back_out.at[s, l], dst_ref=back_in.at[s if arriving else zi, l],
            send_sem=b_send.at[s, l], recv_sem=b_recv.at[s if arriving else zi, l],
            device_id={"dp": s}, device_id_type=MESH)

    def forward_copy(s, o, q, arriving=False):
        j = (xi + o) % m
        at = (j if arriving else xi) * each + q
        return pltpu.make_async_remote_copy(
            src_ref=held.at[s, at], dst_ref=held.at[s, at],
            send_sem=x_send.at[s, j, q], recv_sem=x_recv.at[s, at],
            device_id={"mp": j}, device_id_type=MESH)

    def arrive(o):
        for q in range(each):
            dispatch_copy(o, xi * each + q, True).wait_recv()
            for p in range(1, m):
                forward_copy(partner(o), p, q).start()

    def send_back(s):
        for l in range(tl):
            back_out[s, l] = reduced(s, l)
            back_copy(s, l).start()

    expert_whole(zi)
    tower_sums(zi)

    def work(o, c):
        s = partner(o)
        for q in range(each):
            dispatch_copy(o, xi * each + q).wait_send()
            dispatch_copy(o + 1, xi * each + q).start()
        arrive(o)

        @pl.when(o > 2)
        def _():
            send_back(partner(o - 1))

        expert_own_columns(s)
        expert_other_columns(s)
        tower_sums(s)
        return c

    lax.fori_loop(2, n - 1, work, 0)
    near, last = partner(1), partner(n - 1)
    arrive(n - 1)
    send_back(partner(n - 2))
    for c in range(chunks):
        dispatch_copy(1, c, True).wait_recv()
    expert_whole(near)
    tower_sums(near)
    expert_own_columns(last)
    send_back(near)
    expert_other_columns(last)
    tower_sums(last)
    send_back(last)
    for l in range(tl):
        zsum[l] += jnp.dot(gate[zi], reduced(zi, l), preferred_element_type=F32)

    def collect(s, l):
        back_copy(s, l, True).wait_recv()
        zsum[l] += jnp.dot(gate[s], back_in[s, l], preferred_element_type=F32)

    def collect_step(o, c):
        for l in range(tl):
            collect(partner(o), l)
        return c

    def small_arrive(o, c):
        small_copy(o, True).wait_recv()
        return c

    lax.fori_loop(1, nt, small_arrive, 0)
    cots = [column(small_in[xi * tl + l, 0:1, 0:rows]) for l in range(tl)]
    lax.fori_loop(2, n - 1, collect_step, 0)
    for l in range(tl):
        collect(near, l)

    def pred_copy(l, o):
        y = (xi + o) % m
        return pltpu.make_async_remote_copy(
            src_ref=pred_send.at[l], dst_ref=pred_in.at[ti], send_sem=p_send.at[l, o],
            recv_sem=p_recv.at[ti], device_id={"task": xi * tl + l, "mp": y},
            device_id_type=MESH)

    def dz_copy(l, o, arriving=False):
        j = (xi + o) % m
        at = (j if arriving else xi) * tl + l
        return pltpu.make_async_remote_copy(
            src_ref=dz.at[at], dst_ref=dz.at[at], send_sem=d_send.at[j, l],
            recv_sem=d_recv.at[at], device_id={"mp": j}, device_id_type=MESH)

    for l in range(tl):
        t = xi * tl + l
        collect(last, l)
        z = zsum[l] * scale
        s = sigmoid(z)
        out_row = small_in[t, 1:2, 0:ft]
        dz[t] = (cots[l] * out_row * s * (1.0 + z * (1.0 - s))).astype(BF16)
        for o in range(1, m):
            dz_copy(l, o).start()
        value = jnp.sum(z * s * out_row, axis=1, keepdims=True)
        pred_send[l, 0:1, 0:rows] = jnp.sum(jnp.where(diagonal, value, 0.0), axis=0, keepdims=True)
        mine = ti == t

        @pl.when(mine)
        def _():
            pred_in[ti] = pred_send[l]

        @pl.when(jnp.logical_not(mine))
        def _():
            pred_copy(l, 0).start()

        for o in range(1, m):
            pred_copy(l, o).start()

    def grad(o, c0):
        acc = jnp.zeros((rows, step), F32)
        for l in range(tl):
            t = (xi + o) % m * tl + l
            acc += lax.dot_general(
                dz[t], tw[t, c0:c0 + step, :], (((1,), (1,)), ((), ())),
                preferred_element_type=F32)
        return acc

    for c0 in range(0, units, step):
        gsum[:, c0:c0 + step] = grad(0, c0)
    for o in range(1, m):
        for l in range(tl):
            dz_copy(l, o, True).wait_recv()
    grad_writes = []
    for c0 in range(0, units, step):
        acc = gsum[:, c0:c0 + step]
        for o in range(1, m):
            acc += grad(o, c0)
        block = c0 // step
        gout[block] = acc.astype(BF16)
        grad_writes.append(pltpu.make_async_copy(
            gout.at[block], grad_out.at[:, pl.ds(c0, step)], out_sem.at[block]))
        grad_writes[-1].start()

    keeper = ti // tl
    for k in range(nt):
        @pl.when(jnp.logical_not(jnp.logical_and(keeper == xi, ti == k)))
        def _():
            pltpu.make_async_remote_copy(
                src_ref=pred_send.at[0], dst_ref=pred_in.at[k], send_sem=p_send.at[0, 0],
                recv_sem=p_recv.at[k], device_id={"task": (ti + 1) % nt},
                device_id_type=MESH).wait_recv()

        pred[0:1, k * rows:(k + 1) * rows] = pred_in[k, 0:1, 0:rows]

    pred_write = pltpu.make_async_copy(pred, pred_out, out_sem.at[units // step])
    pred_write.start()

    def drain(o, c):
        s = partner(o)
        for l in range(tl):
            back_copy(s, l).wait_send()
            for p in range(1, m):
                rs_copy(s, p, l).wait_send()
        return c

    def drain_far(o, c):
        for p in range(1, m):
            for q in range(each):
                forward_copy(partner(o), p, q).wait_send()
        return c

    lax.fori_loop(1, n, drain, 0)
    lax.fori_loop(2, n, drain_far, 0)
    for c in range(chunks):
        dispatch_copy(1, c).wait_send()
    for q in range(each):
        dispatch_copy(n - 1, xi * each + q).wait_send()
    for p in range(1, m):
        for l in range(tl):
            rs_copy(zi, p, l).wait_send()
            dz_copy(l, p).wait_send()

    def drain_small(o, c):
        small_copy(o).wait_send()
        return c

    lax.fori_loop(1, nt, drain_small, 0)
    for l in range(tl):
        @pl.when(ti != xi * tl + l)
        def _():
            pred_copy(l, 0).wait_send()

        for o in range(1, m):
            pred_copy(l, o).wait_send()
    for copy in grad_writes:
        copy.wait()
    pred_write.wait()


def body(tokens, expert_ids, gate_levels, expert_weight, tower_weight, tower_out, cotangent):
    n, nt, m = lax.axis_size("dp"), lax.axis_size("task"), lax.axis_size("mp")
    rows, top = expert_ids.shape
    width, units = expert_weight.shape[1:]
    ft = tower_weight.shape[2]
    slots = -(-(5 * rows * top // (4 * n)) // 16) * 16
    depth = width // m
    tl = nt // m
    step = 512 if units % 512 == 0 else units
    wide = -(-max(rows, ft) // 128) * 128
    each = 2
    chunks = m * each
    depth = width // chunks
    hbm = pl.BlockSpec(memory_space=pltpu.HBM)
    dma = pltpu.SemaphoreType.DMA
    return tuple(pl.pallas_call(
        functools.partial(kernel, n, nt, m),
        out_shape=(
            jax.ShapeDtypeStruct((1, nt * rows), F32),
            jax.ShapeDtypeStruct((rows, units), BF16),
        ),
        in_specs=[hbm] * 7,
        out_specs=(hbm, hbm),
        scratch_shapes=[
            pltpu.VMEM((chunks, rows, depth), BF16),
            pltpu.VMEM((width, units), BF16),
            pltpu.VMEM(tower_weight.shape, BF16),
            pltpu.VMEM((top, rows), jnp.int32),
            pltpu.VMEM((top, rows), jnp.int32),
            pltpu.VMEM(tower_out.shape, F32),
            pltpu.VMEM(cotangent.shape, F32),
            pltpu.VMEM((n, chunks, slots, depth), BF16),
            pltpu.VMEM((n, chunks, slots, depth), BF16),
            pltpu.VMEM((n, rows, slots), BF16),
            pltpu.VMEM((slots, units), F32),
            pltpu.VMEM((slots, units), BF16),
            pltpu.VMEM((n, tl, slots, ft), F32),
            pltpu.VMEM((n, m, tl, slots, ft), BF16),
            pltpu.VMEM((n, m, tl, slots, ft), BF16),
            pltpu.VMEM((n, tl, slots, ft), BF16),
            pltpu.VMEM((n, tl, slots, ft), BF16),
            pltpu.VMEM((tl, rows, ft), F32),
            pltpu.VMEM((nt, rows, ft), BF16),
            pltpu.VMEM((rows, units), F32),
            pltpu.VMEM((units // step, rows, step), BF16),
            pltpu.VMEM((1, nt * rows), F32),
            pltpu.VMEM((nt, 8, wide), F32),
            pltpu.VMEM((nt, 8, wide), F32),
            pltpu.VMEM((tl, 8, wide), F32),
            pltpu.VMEM((nt, 8, wide), F32),
            dma((6 + chunks,)),
            dma((n, chunks)), dma((n, chunks)),
            dma((n, m, each)), dma((n, chunks)),
            dma((n, m, tl)), dma((n, m, tl)),
            dma((n, tl)), dma((n, tl)),
            dma((nt,)), dma((nt,)),
            dma((m, tl)), dma((nt,)),
            dma((tl, m)), dma((nt,)), dma((units // step + 1,)),
        ],
        compiler_params=pltpu.CompilerParams(
            collective_id=0, has_side_effects=True, vmem_limit_bytes=60 * 1024 * 1024),
        name="expert_towers",
    )(tokens, expert_ids.T, gate_levels.T, expert_weight, tower_weight, tower_out, cotangent))


def solution(mesh):
    return jax.shard_map(
        body,
        mesh=mesh,
        in_specs=(
            P(("dp", "task"), None),
            P(("dp", "task"), None),
            P(("dp", "task"), None),
            P("dp", None, "mp"),
            P(None, "mp", None),
            P("task", None),
            P("task", "dp"),
        ),
        out_specs=(P("task", "dp"), P(("dp", "task"), "mp")),
        check_vma=False,
    )
```

```python
import functools

import jax
import jax.numpy as jnp
from jax import lax
from jax.experimental import pallas as pl
from jax.experimental.pallas import tpu as pltpu
from jax.sharding import PartitionSpec as P

MESH = pl.DeviceIdType.MESH
F32 = jnp.float32
BF16 = jnp.bfloat16


def sigmoid(v):
    return 0.5 + 0.5 * jnp.tanh(0.5 * v)


def kernel(
    n, nt, m,
    tokens, ids_in, levels_in, weight, towers, tower_out_in, cotangent_in,
    pred_out, grad_out,
    tok, w, tw, ids, levels, tower_out, cotangent,
    disp, held, gate, pre, near_pre, hid, part, rs_out, rs_in, back_out, back_in,
    zsum, dz, gsum, gout, pred, small_out, small_in, pred_send, pred_in,
    load_sem, z_send, z_recv, x_send, x_recv, rs_send, rs_recv, b_send, b_recv,
    s_send, s_recv, d_send, d_recv, p_send, p_recv, out_sem,
):
    zi, ti, xi = lax.axis_index("dp"), lax.axis_index("task"), lax.axis_index("mp")
    rows = ids.shape[1]
    slots = gate.shape[2]
    chunks, _, depth = tok.shape
    each = chunks // m
    units = w.shape[1]
    ft = towers.shape[2]
    tl = nt // m
    step = 512 if units % 512 == 0 else units

    def partner(o):
        other, bit = 0, 1
        while bit < n:
            other = other + bit * ((zi // bit + o // bit) % 2)
            bit *= 2
        return other

    def load(src, dst, i):
        copy = pltpu.make_async_copy(src, dst, load_sem.at[i])
        copy.start()
        return copy

    routing = [load(ids_in, ids, 0), load(levels_in, levels, 1)]
    tok_loads = [
        load(tokens.at[:, pl.ds(c * depth, depth)], tok.at[c], 6 + c) for c in range(chunks)]
    small_loads = [load(tower_out_in, tower_out, 2), load(cotangent_in, cotangent, 3)]
    w_load = load(weight.at[0], w, 4)
    tw_load = load(towers, tw, 5)

    barrier = pltpu.get_barrier_semaphore()

    def greet_line(o, c):
        pl.semaphore_signal(barrier, inc=1, device_id={"dp": partner(o)}, device_id_type=MESH)
        return c

    def greet_plane(o, c):
        at = (ti * m + xi + o) % (nt * m)
        pl.semaphore_signal(
            barrier, inc=1, device_id={"task": at // m, "mp": at % m}, device_id_type=MESH)
        return c

    lax.fori_loop(1, n, greet_line, 0)
    lax.fori_loop(1, nt * m, greet_plane, 0)

    for copy in routing:
        copy.wait()
    names = max(8, n)
    sub = lax.broadcasted_iota(jnp.int32, (names, rows), 0)
    level_of = (
        jnp.where(ids[0:1, :] == sub, levels[0:1, :], 0)
        + jnp.where(ids[1:2, :] == sub, levels[1:2, :], 0)).astype(F32)
    named = jnp.where(level_of > 0, 1.0, 0.0)
    down = lax.broadcasted_iota(jnp.int32, (rows, rows), 0)
    across = lax.broadcasted_iota(jnp.int32, (rows, rows), 1)
    diagonal = down == across
    before = jnp.where(down < across, 1.0, 0.0)
    rank = jnp.dot(named.astype(BF16), before.astype(BF16), preferred_element_type=F32)
    place = jnp.where(named > 0, rank, -1.0)

    def row_of(table, d):
        return jnp.sum(jnp.where(sub == d, table, 0.0), axis=0, keepdims=True)

    def column(row):
        return jnp.sum(jnp.where(diagonal, row, 0.0), axis=1, keepdims=True)

    slot_down = lax.broadcasted_iota(jnp.int32, (slots, rows), 0).astype(F32)
    slot_across = lax.broadcasted_iota(jnp.int32, (rows, slots), 1).astype(F32)

    def pick(d):
        return jnp.where(slot_down == row_of(place, d), 1.0, 0.0).astype(BF16)

    def gathered(spot, c):
        return jnp.dot(spot, tok[c], preferred_element_type=F32).astype(BF16)

    for copy in tok_loads:
        copy.wait()

    def dispatch_copy(o, c, arriving=False):
        d = partner(o)
        return pltpu.make_async_remote_copy(
            src_ref=disp.at[d, c], dst_ref=held.at[d if arriving else zi, c],
            send_sem=z_send.at[d, c], recv_sem=z_recv.at[d if arriving else zi, c],
            device_id={"dp": d}, device_id_type=MESH)

    def fill(o, first, count):
        d = partner(o)
        spot = pick(d)
        for q in range(count):
            disp[d, first + q] = gathered(spot, first + q)

    fill(2, xi * each, each)
    pl.semaphore_wait(barrier, n - 1 + nt * m - 1)
    for q in range(each):
        dispatch_copy(2, xi * each + q).start()
    fill(1, 0, chunks)
    for c in range(chunks):
        dispatch_copy(1, c).start()

    def fill_rest(o, c):
        fill(o, xi * each, each)
        return c

    lax.fori_loop(3, n, fill_rest, 0)

    for copy in small_loads:
        copy.wait()
    for k in range(nt):
        small_out[k, 0:1, 0:rows] = cotangent[0:1, k * rows:(k + 1) * rows]
        small_out[k, 1:2, 0:ft] = tower_out[0:1, :]

    def small_copy(o, arriving=False):
        k = (ti + o) % nt
        return pltpu.make_async_remote_copy(
            src_ref=small_out.at[k], dst_ref=small_in.at[k if arriving else ti],
            send_sem=s_send.at[k], recv_sem=s_recv.at[k if arriving else ti],
            device_id={"task": k}, device_id_type=MESH)

    def send_small(o, c):
        small_copy(o).start()
        return c

    lax.fori_loop(1, nt, send_small, 0)
    small_in[ti] = small_out[ti]

    own = pick(zi)
    for c in range(chunks):
        held[zi, c] = gathered(own, c)

    def set_gate(d, c):
        hit = slot_across == column(row_of(place, d))
        gate[d] = jnp.where(hit, column(row_of(level_of, d)), 0.0).astype(BF16)
        return c

    lax.fori_loop(0, n, set_gate, 0)
    scale = 1.0 / column(jnp.sum(level_of, axis=0, keepdims=True))
    zsum[...] = jnp.zeros_like(zsum)
    w_load.wait()
    tw_load.wait()

    def rs_copy(s, o, l, arriving=False):
        j = (xi + o) % m
        return pltpu.make_async_remote_copy(
            src_ref=rs_out.at[s, j, l], dst_ref=rs_in.at[s, j if arriving else xi, l],
            send_sem=rs_send.at[s, j, l], recv_sem=rs_recv.at[s, j if arriving else xi, l],
            device_id={"mp": j}, device_id_type=MESH)

    def accumulate(sums, s, ats, fresh=False, finish=False):
        for c0 in range(0, units, step):
            acc = jnp.zeros((slots, step), F32) if fresh else sums[:, c0:c0 + step]
            for at in ats:
                acc += jnp.dot(
                    held[s, at], w[pl.ds(pl.multiple_of(at * depth, depth), depth), c0:c0 + step],
                    preferred_element_type=F32)
            if finish:
                hid[:, c0:c0 + step] = (acc * sigmoid(acc)).astype(BF16)
            else:
                sums[:, c0:c0 + step] = acc

    def own_chunk(q):
        return xi * each + q

    def other_chunks(q):
        return [(xi + o) % m * each + q for o in range(1, m)]

    def wait_others(s, q):
        for o in range(1, m):
            forward_copy(s, o, q, True).wait_recv()

    def tower_sums(s):
        for o in range(1, m):
            for l in range(tl):
                j = (xi + o) % m
                u = jnp.dot(hid[...], tw[j * tl + l], preferred_element_type=F32)
                rs_out[s, j, l] = u.astype(BF16)
                rs_copy(s, o, l).start()
        for l in range(tl):
            part[s, l] = jnp.dot(hid[...], tw[xi * tl + l], preferred_element_type=F32)

    def reduced(s, l):
        total = part[s, l]
        for o in range(1, m):
            rs_copy(s, o, l, True).wait_recv()
            total += rs_in[s, (xi + o) % m, l].astype(F32)
        return total.astype(BF16)

    def back_copy(s, l, arriving=False):
        return pltpu.make_async_remote_copy(
            src_ref=back_out.at[s, l], dst_ref=back_in.at[s if arriving else zi, l],
            send_sem=b_send.at[s, l], recv_sem=b_recv.at[s if arriving else zi, l],
            device_id={"dp": s}, device_id_type=MESH)

    def forward_copy(s, o, q, arriving=False):
        j = (xi + o) % m
        at = (j if arriving else xi) * each + q
        return pltpu.make_async_remote_copy(
            src_ref=held.at[s, at], dst_ref=held.at[s, at],
            send_sem=x_send.at[s, j, q], recv_sem=x_recv.at[s, at],
            device_id={"mp": j}, device_id_type=MESH)

    def forward(o, q):
        dispatch_copy(o, own_chunk(q), True).wait_recv()
        for p in range(1, m):
            forward_copy(partner(o), p, q).start()

    def send_back(s):
        for l in range(tl):
            back_out[s, l] = reduced(s, l)
            back_copy(s, l).start()

    accumulate(pre, zi, range(chunks), fresh=True, finish=True)
    tower_sums(zi)

    def work(o, c):
        s = partner(o)
        for q in range(each):
            dispatch_copy(o, own_chunk(q)).wait_send()
            dispatch_copy(o + 1, own_chunk(q)).start()
        for q in range(each):
            forward(o, q)

        @pl.when(o > 2)
        def _():
            send_back(partner(o - 1))

        accumulate(pre, s, [own_chunk(q) for q in range(each)], fresh=True)
        for q in range(each):
            wait_others(s, q)
        accumulate(
            pre, s, [at for q in range(each) for at in other_chunks(q)], finish=True)
        tower_sums(s)
        return c

    lax.fori_loop(2, n - 1, work, 0)

    near, last = partner(1), partner(n - 1)
    cuts = (0, chunks // 2, 3 * chunks // 4, chunks)

    def near_group(g):
        ats = range(cuts[g], cuts[g + 1])
        for at in ats:
            dispatch_copy(1, at, True).wait_recv()
        accumulate(near_pre, near, ats, fresh=g == 0, finish=g == 2)

    forward(n - 1, 0)
    forward(n - 1, 1)
    send_back(partner(n - 2))
    near_group(0)
    forward(n - 1, 2)
    wait_others(last, 0)
    accumulate(pre, last, [own_chunk(0), own_chunk(1)] + other_chunks(0), fresh=True)
    near_group(1)
    forward(n - 1, 3)
    near_group(2)
    tower_sums(near)
    wait_others(last, 1)
    wait_others(last, 2)
    accumulate(
        pre, last, [own_chunk(2), own_chunk(3)] + other_chunks(1) + other_chunks(2))
    send_back(near)
    wait_others(last, 3)
    accumulate(pre, last, other_chunks(3), finish=True)
    tower_sums(last)
    send_back(last)
    for l in range(tl):
        zsum[l] += jnp.dot(gate[zi], reduced(zi, l), preferred_element_type=F32)

    def collect(s, l):
        back_copy(s, l, True).wait_recv()
        zsum[l] += jnp.dot(gate[s], back_in[s, l], preferred_element_type=F32)

    def collect_step(o, c):
        for l in range(tl):
            collect(partner(o), l)
        return c

    def small_arrive(o, c):
        small_copy(o, True).wait_recv()
        return c

    lax.fori_loop(1, nt, small_arrive, 0)
    cots = [column(small_in[xi * tl + l, 0:1, 0:rows]) for l in range(tl)]
    lax.fori_loop(2, n - 1, collect_step, 0)
    for l in range(tl):
        collect(near, l)

    def pred_copy(l, o):
        y = (xi + o) % m
        return pltpu.make_async_remote_copy(
            src_ref=pred_send.at[l], dst_ref=pred_in.at[ti], send_sem=p_send.at[l, o],
            recv_sem=p_recv.at[ti], device_id={"task": xi * tl + l, "mp": y},
            device_id_type=MESH)

    def dz_copy(l, o, arriving=False):
        j = (xi + o) % m
        at = (j if arriving else xi) * tl + l
        return pltpu.make_async_remote_copy(
            src_ref=dz.at[at], dst_ref=dz.at[at], send_sem=d_send.at[j, l],
            recv_sem=d_recv.at[at], device_id={"mp": j}, device_id_type=MESH)

    for l in range(tl):
        t = xi * tl + l
        collect(last, l)
        z = zsum[l] * scale
        s = sigmoid(z)
        out_row = small_in[t, 1:2, 0:ft]
        dz[t] = (cots[l] * out_row * s * (1.0 + z * (1.0 - s))).astype(BF16)
        for o in range(1, m):
            dz_copy(l, o).start()
        value = jnp.sum(z * s * out_row, axis=1, keepdims=True)
        pred_send[l, 0:1, 0:rows] = jnp.sum(jnp.where(diagonal, value, 0.0), axis=0, keepdims=True)
        mine = ti == t

        @pl.when(mine)
        def _():
            pred_in[ti] = pred_send[l]

        @pl.when(jnp.logical_not(mine))
        def _():
            pred_copy(l, 0).start()

        for o in range(1, m):
            pred_copy(l, o).start()

    def grad(o, c0):
        acc = jnp.zeros((rows, step), F32)
        for l in range(tl):
            t = (xi + o) % m * tl + l
            acc += lax.dot_general(
                dz[t], tw[t, c0:c0 + step, :], (((1,), (1,)), ((), ())),
                preferred_element_type=F32)
        return acc

    for c0 in range(0, units, step):
        gsum[:, c0:c0 + step] = grad(0, c0)
    for o in range(1, m):
        for l in range(tl):
            dz_copy(l, o, True).wait_recv()
    grad_writes = []
    for c0 in range(0, units, step):
        acc = gsum[:, c0:c0 + step]
        for o in range(1, m):
            acc += grad(o, c0)
        block = c0 // step
        gout[block] = acc.astype(BF16)
        grad_writes.append(pltpu.make_async_copy(
            gout.at[block], grad_out.at[:, pl.ds(c0, step)], out_sem.at[block]))
        grad_writes[-1].start()

    keeper = ti // tl
    for k in range(nt):
        @pl.when(jnp.logical_not(jnp.logical_and(keeper == xi, ti == k)))
        def _():
            pltpu.make_async_remote_copy(
                src_ref=pred_send.at[0], dst_ref=pred_in.at[k], send_sem=p_send.at[0, 0],
                recv_sem=p_recv.at[k], device_id={"task": (ti + 1) % nt},
                device_id_type=MESH).wait_recv()

        pred[0:1, k * rows:(k + 1) * rows] = pred_in[k, 0:1, 0:rows]

    pred_write = pltpu.make_async_copy(pred, pred_out, out_sem.at[units // step])
    pred_write.start()

    def drain(o, c):
        s = partner(o)
        for l in range(tl):
            back_copy(s, l).wait_send()
            for p in range(1, m):
                rs_copy(s, p, l).wait_send()
        return c

    def drain_far(o, c):
        for p in range(1, m):
            for q in range(each):
                forward_copy(partner(o), p, q).wait_send()
        return c

    lax.fori_loop(1, n, drain, 0)
    lax.fori_loop(2, n, drain_far, 0)
    for c in range(chunks):
        dispatch_copy(1, c).wait_send()
    for q in range(each):
        dispatch_copy(n - 1, xi * each + q).wait_send()
    for p in range(1, m):
        for l in range(tl):
            rs_copy(zi, p, l).wait_send()
            dz_copy(l, p).wait_send()

    def drain_small(o, c):
        small_copy(o).wait_send()
        return c

    lax.fori_loop(1, nt, drain_small, 0)
    for l in range(tl):
        @pl.when(ti != xi * tl + l)
        def _():
            pred_copy(l, 0).wait_send()

        for o in range(1, m):
            pred_copy(l, o).wait_send()
    for copy in grad_writes:
        copy.wait()
    pred_write.wait()


def hand_over(pred, grad, pred_out, grad_out, sem):
    rows = grad.shape[0] // 4
    copies = [pltpu.make_async_copy(pred, pred_out, sem.at[4])]
    for i in range(4):
        at = pl.ds(i * rows, rows)
        copies.append(pltpu.make_async_copy(grad.at[at, :], grad_out.at[at, :], sem.at[i]))
    for copy in copies:
        copy.start()
    for copy in copies:
        copy.wait()


def body(tokens, expert_ids, gate_levels, expert_weight, tower_weight, tower_out, cotangent):
    n, nt, m = lax.axis_size("dp"), lax.axis_size("task"), lax.axis_size("mp")
    rows, top = expert_ids.shape
    width, units = expert_weight.shape[1:]
    ft = tower_weight.shape[2]
    slots = -(-(5 * rows * top // (4 * n)) // 16) * 16
    depth = width // m
    tl = nt // m
    step = 512 if units % 512 == 0 else units
    wide = -(-max(rows, ft) // 128) * 128
    each = 4
    chunks = m * each
    depth = width // chunks
    hbm = pl.BlockSpec(memory_space=pltpu.HBM)
    dma = pltpu.SemaphoreType.DMA
    pred, grad = pl.pallas_call(
        functools.partial(kernel, n, nt, m),
        out_shape=(
            jax.ShapeDtypeStruct((1, nt * rows), F32),
            jax.ShapeDtypeStruct((rows, units), BF16),
        ),
        in_specs=[hbm] * 7,
        out_specs=(hbm, hbm),
        scratch_shapes=[
            pltpu.VMEM((chunks, rows, depth), BF16),
            pltpu.VMEM((width, units), BF16),
            pltpu.VMEM(tower_weight.shape, BF16),
            pltpu.VMEM((top, rows), jnp.int32),
            pltpu.VMEM((top, rows), jnp.int32),
            pltpu.VMEM(tower_out.shape, F32),
            pltpu.VMEM(cotangent.shape, F32),
            pltpu.VMEM((n, chunks, slots, depth), BF16),
            pltpu.VMEM((n, chunks, slots, depth), BF16),
            pltpu.VMEM((n, rows, slots), BF16),
            pltpu.VMEM((slots, units), F32),
            pltpu.VMEM((slots, units), F32),
            pltpu.VMEM((slots, units), BF16),
            pltpu.VMEM((n, tl, slots, ft), F32),
            pltpu.VMEM((n, m, tl, slots, ft), BF16),
            pltpu.VMEM((n, m, tl, slots, ft), BF16),
            pltpu.VMEM((n, tl, slots, ft), BF16),
            pltpu.VMEM((n, tl, slots, ft), BF16),
            pltpu.VMEM((tl, rows, ft), F32),
            pltpu.VMEM((nt, rows, ft), BF16),
            pltpu.VMEM((rows, units), F32),
            pltpu.VMEM((units // step, rows, step), BF16),
            pltpu.VMEM((1, nt * rows), F32),
            pltpu.VMEM((nt, 8, wide), F32),
            pltpu.VMEM((nt, 8, wide), F32),
            pltpu.VMEM((tl, 8, wide), F32),
            pltpu.VMEM((nt, 8, wide), F32),
            dma((6 + chunks,)),
            dma((n, chunks)), dma((n, chunks)),
            dma((n, m, each)), dma((n, chunks)),
            dma((n, m, tl)), dma((n, m, tl)),
            dma((n, tl)), dma((n, tl)),
            dma((nt,)), dma((nt,)),
            dma((m, tl)), dma((nt,)),
            dma((tl, m)), dma((nt,)), dma((units // step + 1,)),
        ],
        compiler_params=pltpu.CompilerParams(
            collective_id=0, has_side_effects=True, vmem_limit_bytes=60 * 1024 * 1024),
        name="expert_towers",
    )(tokens, expert_ids.T, gate_levels.T, expert_weight, tower_weight, tower_out, cotangent)
    return tuple(pl.pallas_call(
        hand_over,
        out_shape=(
            jax.ShapeDtypeStruct(pred.shape, F32),
            jax.ShapeDtypeStruct(grad.shape, BF16),
        ),
        in_specs=[hbm] * 2,
        out_specs=(hbm, hbm),
        scratch_shapes=[dma((5,))],
        compiler_params=pltpu.CompilerParams(vmem_limit_bytes=60 * 1024 * 1024),
        name="hand_over",
    )(pred, grad))


def solution(mesh):
    return jax.shard_map(
        body,
        mesh=mesh,
        in_specs=(
            P(("dp", "task"), None),
            P(("dp", "task"), None),
            P(("dp", "task"), None),
            P("dp", None, "mp"),
            P(None, "mp", None),
            P("task", None),
            P("task", "dp"),
        ),
        out_specs=(P("task", "dp"), P(("dp", "task"), "mp")),
        check_vma=False,
    )
```

```python
import functools

import jax
import jax.numpy as jnp
from jax import lax
from jax.experimental import pallas as pl
from jax.experimental.pallas import tpu as pltpu
from jax.sharding import PartitionSpec as P

MESH = pl.DeviceIdType.MESH
F32 = jnp.float32
BF16 = jnp.bfloat16


def sigmoid(v):
    return 0.5 + 0.5 * jnp.tanh(0.5 * v)


def kernel(
    n, nt, m,
    tokens, ids_in, levels_in, weight, towers, tower_out_in, cotangent_in,
    pred_out, grad_out,
    tok, w, tw, ids, levels, tower_out, cotangent,
    disp, held, gate, pre, near_pre, hid, part, rs_out, rs_in, back_out, back_in,
    zsum, dz, gsum, gout, pred, small_out, small_in, pred_send, pred_in,
    load_sem, z_send, z_recv, x_send, x_recv, rs_send, rs_recv, b_send, b_recv,
    s_send, s_recv, d_send, d_recv, p_send, p_recv, out_sem,
):
    zi, ti, xi = lax.axis_index("dp"), lax.axis_index("task"), lax.axis_index("mp")
    rows = ids.shape[1]
    slots = gate.shape[2]
    chunks, _, depth = tok.shape
    each = chunks // m
    units = w.shape[1]
    ft = towers.shape[2]
    tl = nt // m
    step = 512 if units % 512 == 0 else units

    def partner(o):
        other, bit = 0, 1
        while bit < n:
            other = other + bit * ((zi // bit + o // bit) % 2)
            bit *= 2
        return other

    def load(src, dst, i):
        copy = pltpu.make_async_copy(src, dst, load_sem.at[i])
        copy.start()
        return copy

    routing = [load(ids_in, ids, 0), load(levels_in, levels, 1)]
    tok_loads = [
        load(tokens.at[:, pl.ds(c * depth, depth)], tok.at[c], 6 + c) for c in range(chunks)]
    small_loads = [load(tower_out_in, tower_out, 2), load(cotangent_in, cotangent, 3)]
    w_load = load(weight.at[0], w, 4)
    tw_load = load(towers, tw, 5)

    barrier = pltpu.get_barrier_semaphore()

    def greet_line(o, c):
        pl.semaphore_signal(barrier, inc=1, device_id={"dp": partner(o)}, device_id_type=MESH)
        return c

    def greet_plane(o, c):
        at = (ti * m + xi + o) % (nt * m)
        pl.semaphore_signal(
            barrier, inc=1, device_id={"task": at // m, "mp": at % m}, device_id_type=MESH)
        return c

    lax.fori_loop(1, n, greet_line, 0)
    lax.fori_loop(1, nt * m, greet_plane, 0)

    for copy in routing:
        copy.wait()
    names = max(8, n)
    sub = lax.broadcasted_iota(jnp.int32, (names, rows), 0)
    level_of = (
        jnp.where(ids[0:1, :] == sub, levels[0:1, :], 0)
        + jnp.where(ids[1:2, :] == sub, levels[1:2, :], 0)).astype(F32)
    named = jnp.where(level_of > 0, 1.0, 0.0)
    down = lax.broadcasted_iota(jnp.int32, (rows, rows), 0)
    across = lax.broadcasted_iota(jnp.int32, (rows, rows), 1)
    diagonal = down == across
    before = jnp.where(down < across, 1.0, 0.0)
    rank = jnp.dot(named.astype(BF16), before.astype(BF16), preferred_element_type=F32)
    place = jnp.where(named > 0, rank, -1.0)

    def row_of(table, d):
        return jnp.sum(jnp.where(sub == d, table, 0.0), axis=0, keepdims=True)

    def column(row):
        return jnp.sum(jnp.where(diagonal, row, 0.0), axis=1, keepdims=True)

    slot_down = lax.broadcasted_iota(jnp.int32, (slots, rows), 0).astype(F32)
    slot_across = lax.broadcasted_iota(jnp.int32, (rows, slots), 1).astype(F32)

    def pick(d):
        return jnp.where(slot_down == row_of(place, d), 1.0, 0.0).astype(BF16)

    def gathered(spot, c):
        return jnp.dot(spot, tok[c], preferred_element_type=F32).astype(BF16)

    for copy in tok_loads:
        copy.wait()

    def dispatch_copy(o, c, arriving=False):
        d = partner(o)
        return pltpu.make_async_remote_copy(
            src_ref=disp.at[d, c], dst_ref=held.at[d if arriving else zi, c],
            send_sem=z_send.at[d, c], recv_sem=z_recv.at[d if arriving else zi, c],
            device_id={"dp": d}, device_id_type=MESH)

    def fill(o, first, count):
        d = partner(o)
        spot = pick(d)
        for q in range(count):
            disp[d, first + q] = gathered(spot, first + q)

    fill(2, xi * each, each)
    pl.semaphore_wait(barrier, n - 1 + nt * m - 1)
    dispatch_copy(2, xi * each).start()
    fill(1, 0, chunks)
    for q in range(each):
        if q > 0:
            dispatch_copy(2, xi * each + q).start()
        dispatch_copy(1, q).start()

    def fill_rest(o, c):
        fill(o, xi * each, each)
        return c

    lax.fori_loop(3, n, fill_rest, 0)

    for copy in small_loads:
        copy.wait()
    for k in range(nt):
        small_out[k, 0:1, 0:rows] = cotangent[0:1, k * rows:(k + 1) * rows]
        small_out[k, 1:2, 0:ft] = tower_out[0:1, :]

    def small_copy(o, arriving=False):
        k = (ti + o) % nt
        return pltpu.make_async_remote_copy(
            src_ref=small_out.at[k], dst_ref=small_in.at[k if arriving else ti],
            send_sem=s_send.at[k], recv_sem=s_recv.at[k if arriving else ti],
            device_id={"task": k}, device_id_type=MESH)

    def send_small(o, c):
        small_copy(o).start()
        return c

    lax.fori_loop(1, nt, send_small, 0)
    small_in[ti] = small_out[ti]

    own = pick(zi)
    for c in range(chunks):
        held[zi, c] = gathered(own, c)

    def set_gate(d, c):
        hit = slot_across == column(row_of(place, d))
        gate[d] = jnp.where(hit, column(row_of(level_of, d)), 0.0).astype(BF16)
        return c

    lax.fori_loop(0, n, set_gate, 0)
    scale = 1.0 / column(jnp.sum(level_of, axis=0, keepdims=True))
    zsum[...] = jnp.zeros_like(zsum)
    w_load.wait()
    tw_load.wait()

    def rs_copy(s, o, l, arriving=False):
        j = (xi + o) % m
        return pltpu.make_async_remote_copy(
            src_ref=rs_out.at[s, j, l], dst_ref=rs_in.at[s, j if arriving else xi, l],
            send_sem=rs_send.at[s, j, l], recv_sem=rs_recv.at[s, j if arriving else xi, l],
            device_id={"mp": j}, device_id_type=MESH)

    def accumulate(sums, s, ats, fresh=False, finish=False):
        for c0 in range(0, units, step):
            acc = jnp.zeros((slots, step), F32) if fresh else sums[:, c0:c0 + step]
            for at in ats:
                acc += jnp.dot(
                    held[s, at], w[pl.ds(pl.multiple_of(at * depth, depth), depth), c0:c0 + step],
                    preferred_element_type=F32)
            if finish:
                hid[:, c0:c0 + step] = (acc * sigmoid(acc)).astype(BF16)
            else:
                sums[:, c0:c0 + step] = acc

    def own_chunk(q):
        return xi * each + q

    def other_chunks(q):
        return [(xi + o) % m * each + q for o in range(1, m)]

    def wait_others(s, q):
        for o in range(1, m):
            forward_copy(s, o, q, True).wait_recv()

    def tower_sums(s):
        for o in range(1, m):
            for l in range(tl):
                j = (xi + o) % m
                u = jnp.dot(hid[...], tw[j * tl + l], preferred_element_type=F32)
                rs_out[s, j, l] = u.astype(BF16)
                rs_copy(s, o, l).start()
        for l in range(tl):
            part[s, l] = jnp.dot(hid[...], tw[xi * tl + l], preferred_element_type=F32)

    def reduced(s, l):
        total = part[s, l]
        for o in range(1, m):
            rs_copy(s, o, l, True).wait_recv()
            total += rs_in[s, (xi + o) % m, l].astype(F32)
        return total.astype(BF16)

    def back_copy(s, l, arriving=False):
        return pltpu.make_async_remote_copy(
            src_ref=back_out.at[s, l], dst_ref=back_in.at[s if arriving else zi, l],
            send_sem=b_send.at[s, l], recv_sem=b_recv.at[s if arriving else zi, l],
            device_id={"dp": s}, device_id_type=MESH)

    def forward_copy(s, o, q, arriving=False):
        j = (xi + o) % m
        at = (j if arriving else xi) * each + q
        return pltpu.make_async_remote_copy(
            src_ref=held.at[s, at], dst_ref=held.at[s, at],
            send_sem=x_send.at[s, j, q], recv_sem=x_recv.at[s, at],
            device_id={"mp": j}, device_id_type=MESH)

    def forward(o, q):
        dispatch_copy(o, own_chunk(q), True).wait_recv()
        for p in range(1, m):
            forward_copy(partner(o), p, q).start()

    def send_back(s):
        for l in range(tl):
            back_out[s, l] = reduced(s, l)
            back_copy(s, l).start()

    accumulate(pre, zi, range(chunks), fresh=True, finish=True)
    for q in range(each):
        dispatch_copy(3, own_chunk(q)).start()
        for c in range(each + q * (m - 1), each + (q + 1) * (m - 1)):
            dispatch_copy(1, c).start()
    forward(2, 0)
    tower_sums(zi)
    forward(2, 1)

    def work(o, c):
        s = partner(o)

        @pl.when(o + 2 < n)
        def _():
            for q in range(each):
                dispatch_copy(o, own_chunk(q)).wait_send()
                dispatch_copy(o + 2, own_chunk(q)).start()

        @pl.when(o > 2)
        def _():
            forward(o, 0)
            forward(o, 1)

        forward(o, 2)
        forward(o, 3)

        @pl.when(o > 2)
        def _():
            send_back(partner(o - 1))

        accumulate(pre, s, [own_chunk(q) for q in range(each)], fresh=True)
        for q in range(each):
            wait_others(s, q)
        accumulate(
            pre, s, [at for q in range(each) for at in other_chunks(q)], finish=True)
        tower_sums(s)
        return c

    lax.fori_loop(2, n - 1, work, 0)

    near, last = partner(1), partner(n - 1)
    cuts = (0, chunks // 2, 3 * chunks // 4, chunks)

    def near_group(g):
        ats = range(cuts[g], cuts[g + 1])
        for at in ats:
            dispatch_copy(1, at, True).wait_recv()
        accumulate(near_pre, near, ats, fresh=g == 0, finish=g == 2)

    forward(n - 1, 0)
    forward(n - 1, 1)
    send_back(partner(n - 2))
    near_group(0)
    forward(n - 1, 2)
    wait_others(last, 0)
    accumulate(pre, last, [own_chunk(0), own_chunk(1)] + other_chunks(0), fresh=True)
    near_group(1)
    forward(n - 1, 3)
    near_group(2)
    tower_sums(near)
    wait_others(last, 1)
    wait_others(last, 2)
    accumulate(
        pre, last, [own_chunk(2), own_chunk(3)] + other_chunks(1) + other_chunks(2))
    send_back(near)
    wait_others(last, 3)
    accumulate(pre, last, other_chunks(3), finish=True)
    tower_sums(last)
    send_back(last)
    for l in range(tl):
        zsum[l] += jnp.dot(gate[zi], reduced(zi, l), preferred_element_type=F32)

    def collect(s, l):
        back_copy(s, l, True).wait_recv()
        zsum[l] += jnp.dot(gate[s], back_in[s, l], preferred_element_type=F32)

    def collect_step(o, c):
        for l in range(tl):
            collect(partner(o), l)
        return c

    def small_arrive(o, c):
        small_copy(o, True).wait_recv()
        return c

    lax.fori_loop(1, nt, small_arrive, 0)
    cots = [column(small_in[xi * tl + l, 0:1, 0:rows]) for l in range(tl)]
    lax.fori_loop(2, n - 1, collect_step, 0)
    for l in range(tl):
        collect(near, l)

    def pred_copy(l, o):
        y = (xi + o) % m
        return pltpu.make_async_remote_copy(
            src_ref=pred_send.at[l], dst_ref=pred_in.at[ti], send_sem=p_send.at[l, o],
            recv_sem=p_recv.at[ti], device_id={"task": xi * tl + l, "mp": y},
            device_id_type=MESH)

    def dz_copy(l, o, arriving=False):
        j = (xi + o) % m
        at = (j if arriving else xi) * tl + l
        return pltpu.make_async_remote_copy(
            src_ref=dz.at[at], dst_ref=dz.at[at], send_sem=d_send.at[j, l],
            recv_sem=d_recv.at[at], device_id={"mp": j}, device_id_type=MESH)

    for l in range(tl):
        t = xi * tl + l
        collect(last, l)
        z = zsum[l] * scale
        s = sigmoid(z)
        out_row = small_in[t, 1:2, 0:ft]
        dz[t] = (cots[l] * out_row * s * (1.0 + z * (1.0 - s))).astype(BF16)
        for o in range(1, m):
            dz_copy(l, o).start()
        value = jnp.sum(z * s * out_row, axis=1, keepdims=True)
        pred_send[l, 0:1, 0:rows] = jnp.sum(jnp.where(diagonal, value, 0.0), axis=0, keepdims=True)
        mine = ti == t

        @pl.when(mine)
        def _():
            pred_in[ti] = pred_send[l]

        @pl.when(jnp.logical_not(mine))
        def _():
            pred_copy(l, 0).start()

        for o in range(1, m):
            pred_copy(l, o).start()

    def grad(o, c0):
        acc = jnp.zeros((rows, step), F32)
        for l in range(tl):
            t = (xi + o) % m * tl + l
            acc += lax.dot_general(
                dz[t], tw[t, c0:c0 + step, :], (((1,), (1,)), ((), ())),
                preferred_element_type=F32)
        return acc

    for c0 in range(0, units, step):
        gsum[:, c0:c0 + step] = grad(0, c0)
    for o in range(1, m):
        for l in range(tl):
            dz_copy(l, o, True).wait_recv()
    grad_writes = []
    for c0 in range(0, units, step):
        acc = gsum[:, c0:c0 + step]
        for o in range(1, m):
            acc += grad(o, c0)
        block = c0 // step
        gout[block] = acc.astype(BF16)
        grad_writes.append(pltpu.make_async_copy(
            gout.at[block], grad_out.at[:, pl.ds(c0, step)], out_sem.at[block]))
        grad_writes[-1].start()

    keeper = ti // tl
    for k in range(nt):
        @pl.when(jnp.logical_not(jnp.logical_and(keeper == xi, ti == k)))
        def _():
            pltpu.make_async_remote_copy(
                src_ref=pred_send.at[0], dst_ref=pred_in.at[k], send_sem=p_send.at[0, 0],
                recv_sem=p_recv.at[k], device_id={"task": (ti + 1) % nt},
                device_id_type=MESH).wait_recv()

        pred[0:1, k * rows:(k + 1) * rows] = pred_in[k, 0:1, 0:rows]

    pred_write = pltpu.make_async_copy(pred, pred_out, out_sem.at[units // step])
    pred_write.start()

    def drain(o, c):
        s = partner(o)
        for l in range(tl):
            back_copy(s, l).wait_send()
            for p in range(1, m):
                rs_copy(s, p, l).wait_send()
        return c

    def drain_far(o, c):
        for p in range(1, m):
            for q in range(each):
                forward_copy(partner(o), p, q).wait_send()
        return c

    lax.fori_loop(1, n, drain, 0)
    lax.fori_loop(2, n, drain_far, 0)
    for c in range(chunks):
        dispatch_copy(1, c).wait_send()
    for q in range(each):
        dispatch_copy(n - 2, xi * each + q).wait_send()
        dispatch_copy(n - 1, xi * each + q).wait_send()
    for p in range(1, m):
        for l in range(tl):
            rs_copy(zi, p, l).wait_send()
            dz_copy(l, p).wait_send()

    def drain_small(o, c):
        small_copy(o).wait_send()
        return c

    lax.fori_loop(1, nt, drain_small, 0)
    for l in range(tl):
        @pl.when(ti != xi * tl + l)
        def _():
            pred_copy(l, 0).wait_send()

        for o in range(1, m):
            pred_copy(l, o).wait_send()
    for copy in grad_writes:
        copy.wait()
    pred_write.wait()


def hand_over(pred, grad, pred_out, grad_out, pred_here, grad_here, sem):
    rows = grad.shape[0] // 4
    parts = [(pred, pred_here, pred_out)]
    for i in range(4):
        at = pl.ds(i * rows, rows)
        parts.append((grad.at[at, :], grad_here.at[at, :], grad_out.at[at, :]))
    reads = [pltpu.make_async_copy(a, b, sem.at[0, i]) for i, (a, b, _) in enumerate(parts)]
    writes = [pltpu.make_async_copy(b, c, sem.at[1, i]) for i, (_, b, c) in enumerate(parts)]
    for read in reads:
        read.start()
    for read, write in zip(reads, writes):
        read.wait()
        write.start()
    for write in writes:
        write.wait()


def body(tokens, expert_ids, gate_levels, expert_weight, tower_weight, tower_out, cotangent):
    n, nt, m = lax.axis_size("dp"), lax.axis_size("task"), lax.axis_size("mp")
    rows, top = expert_ids.shape
    width, units = expert_weight.shape[1:]
    ft = tower_weight.shape[2]
    slots = -(-(5 * rows * top // (4 * n)) // 16) * 16
    depth = width // m
    tl = nt // m
    step = 512 if units % 512 == 0 else units
    wide = -(-max(rows, ft) // 128) * 128
    each = 4
    chunks = m * each
    depth = width // chunks
    hbm = pl.BlockSpec(memory_space=pltpu.HBM)
    dma = pltpu.SemaphoreType.DMA
    pred, grad = pl.pallas_call(
        functools.partial(kernel, n, nt, m),
        out_shape=(
            jax.ShapeDtypeStruct((1, nt * rows), F32),
            jax.ShapeDtypeStruct((rows, units), BF16),
        ),
        in_specs=[hbm] * 7,
        out_specs=(hbm, hbm),
        scratch_shapes=[
            pltpu.VMEM((chunks, rows, depth), BF16),
            pltpu.VMEM((width, units), BF16),
            pltpu.VMEM(tower_weight.shape, BF16),
            pltpu.VMEM((top, rows), jnp.int32),
            pltpu.VMEM((top, rows), jnp.int32),
            pltpu.VMEM(tower_out.shape, F32),
            pltpu.VMEM(cotangent.shape, F32),
            pltpu.VMEM((n, chunks, slots, depth), BF16),
            pltpu.VMEM((n, chunks, slots, depth), BF16),
            pltpu.VMEM((n, rows, slots), BF16),
            pltpu.VMEM((slots, units), F32),
            pltpu.VMEM((slots, units), F32),
            pltpu.VMEM((slots, units), BF16),
            pltpu.VMEM((n, tl, slots, ft), F32),
            pltpu.VMEM((n, m, tl, slots, ft), BF16),
            pltpu.VMEM((n, m, tl, slots, ft), BF16),
            pltpu.VMEM((n, tl, slots, ft), BF16),
            pltpu.VMEM((n, tl, slots, ft), BF16),
            pltpu.VMEM((tl, rows, ft), F32),
            pltpu.VMEM((nt, rows, ft), BF16),
            pltpu.VMEM((rows, units), F32),
            pltpu.VMEM((units // step, rows, step), BF16),
            pltpu.VMEM((1, nt * rows), F32),
            pltpu.VMEM((nt, 8, wide), F32),
            pltpu.VMEM((nt, 8, wide), F32),
            pltpu.VMEM((tl, 8, wide), F32),
            pltpu.VMEM((nt, 8, wide), F32),
            dma((6 + chunks,)),
            dma((n, chunks)), dma((n, chunks)),
            dma((n, m, each)), dma((n, chunks)),
            dma((n, m, tl)), dma((n, m, tl)),
            dma((n, tl)), dma((n, tl)),
            dma((nt,)), dma((nt,)),
            dma((m, tl)), dma((nt,)),
            dma((tl, m)), dma((nt,)), dma((units // step + 1,)),
        ],
        compiler_params=pltpu.CompilerParams(
            collective_id=0, has_side_effects=True, vmem_limit_bytes=60 * 1024 * 1024),
        name="expert_towers",
    )(tokens, expert_ids.T, gate_levels.T, expert_weight, tower_weight, tower_out, cotangent)
    return tuple(pl.pallas_call(
        hand_over,
        out_shape=(
            jax.ShapeDtypeStruct(pred.shape, F32),
            jax.ShapeDtypeStruct(grad.shape, BF16),
        ),
        in_specs=[hbm] * 2,
        out_specs=(hbm, hbm),
        scratch_shapes=[
            pltpu.VMEM(pred.shape, F32), pltpu.VMEM(grad.shape, BF16), dma((2, 5))],
        compiler_params=pltpu.CompilerParams(vmem_limit_bytes=60 * 1024 * 1024),
        name="hand_over",
    )(pred, grad))


def solution(mesh):
    return jax.shard_map(
        body,
        mesh=mesh,
        in_specs=(
            P(("dp", "task"), None),
            P(("dp", "task"), None),
            P(("dp", "task"), None),
            P("dp", None, "mp"),
            P(None, "mp", None),
            P("task", None),
            P("task", "dp"),
        ),
        out_specs=(P("task", "dp"), P(("dp", "task"), "mp")),
        check_vma=False,
    )
```

```python
import functools

import jax
import jax.numpy as jnp
from jax import lax
from jax.experimental import pallas as pl
from jax.experimental.pallas import tpu as pltpu
from jax.sharding import PartitionSpec as P

MESH = pl.DeviceIdType.MESH
F32 = jnp.float32
BF16 = jnp.bfloat16


def sigmoid(v):
    return 0.5 + 0.5 * jnp.tanh(0.5 * v)


def kernel(
    n, nt, m,
    tokens, ids_in, levels_in, weight, towers, tower_out_in, cotangent_in,
    pred_out, grad_out,
    tok, w, tw, ids, levels, tower_out, cotangent,
    disp, held, gate, pre, near_pre, hid, part, rs_out, rs_in, back_out, back_in,
    zsum, dz, gsum, gout, pred, small_out, small_in, pred_send, pred_in,
    load_sem, z_send, z_recv, x_send, x_recv, rs_send, rs_recv, b_send, b_recv,
    s_send, s_recv, d_send, d_recv, p_send, p_recv, out_sem,
):
    zi, ti, xi = lax.axis_index("dp"), lax.axis_index("task"), lax.axis_index("mp")
    rows = ids.shape[1]
    slots = gate.shape[2]
    chunks, _, depth = tok.shape
    each = chunks // m
    units = w.shape[1]
    ft = towers.shape[2]
    tl = nt // m
    step = 512 if units % 512 == 0 else units

    def partner(o):
        other, bit = 0, 1
        while bit < n:
            other = other + bit * ((zi // bit + o // bit) % 2)
            bit *= 2
        return other

    def load(src, dst, i):
        copy = pltpu.make_async_copy(src, dst, load_sem.at[i])
        copy.start()
        return copy

    routing = [load(ids_in, ids, 0), load(levels_in, levels, 1)]
    tok_loads = [
        load(tokens.at[:, pl.ds(c * depth, depth)], tok.at[c], 6 + c) for c in range(chunks)]
    small_loads = [load(tower_out_in, tower_out, 2), load(cotangent_in, cotangent, 3)]
    w_load = load(weight.at[0], w, 4)
    tw_load = load(towers, tw, 5)

    barrier = pltpu.get_barrier_semaphore()

    def greet_line(o, c):
        pl.semaphore_signal(barrier, inc=1, device_id={"dp": partner(o)}, device_id_type=MESH)
        return c

    def greet_plane(o, c):
        at = (ti * m + xi + o) % (nt * m)
        pl.semaphore_signal(
            barrier, inc=1, device_id={"task": at // m, "mp": at % m}, device_id_type=MESH)
        return c

    lax.fori_loop(1, n, greet_line, 0)
    lax.fori_loop(1, nt * m, greet_plane, 0)

    for copy in routing:
        copy.wait()
    names = max(8, n)
    sub = lax.broadcasted_iota(jnp.int32, (names, rows), 0)
    level_of = (
        jnp.where(ids[0:1, :] == sub, levels[0:1, :], 0)
        + jnp.where(ids[1:2, :] == sub, levels[1:2, :], 0)).astype(F32)
    named = jnp.where(level_of > 0, 1.0, 0.0)
    down = lax.broadcasted_iota(jnp.int32, (rows, rows), 0)
    across = lax.broadcasted_iota(jnp.int32, (rows, rows), 1)
    diagonal = down == across
    before = jnp.where(down < across, 1.0, 0.0)
    rank = jnp.dot(named.astype(BF16), before.astype(BF16), preferred_element_type=F32)
    place = jnp.where(named > 0, rank, -1.0)

    def row_of(table, d):
        return jnp.sum(jnp.where(sub == d, table, 0.0), axis=0, keepdims=True)

    def column(row):
        return jnp.sum(jnp.where(diagonal, row, 0.0), axis=1, keepdims=True)

    slot_down = lax.broadcasted_iota(jnp.int32, (slots, rows), 0).astype(F32)
    slot_across = lax.broadcasted_iota(jnp.int32, (rows, slots), 1).astype(F32)

    def pick(d):
        return jnp.where(slot_down == row_of(place, d), 1.0, 0.0).astype(BF16)

    def gathered(spot, c):
        return jnp.dot(spot, tok[c], preferred_element_type=F32).astype(BF16)

    for copy in tok_loads:
        copy.wait()

    def dispatch_copy(o, c, arriving=False):
        d = partner(o)
        return pltpu.make_async_remote_copy(
            src_ref=disp.at[d, c], dst_ref=held.at[d if arriving else zi, c],
            send_sem=z_send.at[d, c], recv_sem=z_recv.at[d if arriving else zi, c],
            device_id={"dp": d}, device_id_type=MESH)

    def fill(o, first, count):
        d = partner(o)
        spot = pick(d)
        for q in range(count):
            disp[d, first + q] = gathered(spot, first + q)

    fill(2, xi * each, each)
    pl.semaphore_wait(barrier, n - 1 + nt * m - 1)
    dispatch_copy(2, xi * each).start()
    fill(1, 0, chunks)
    for q in range(each):
        if q > 0:
            dispatch_copy(2, xi * each + q).start()
        dispatch_copy(1, q).start()

    def fill_rest(o, c):
        fill(o, xi * each, each)
        return c

    lax.fori_loop(3, n, fill_rest, 0)
    for q in range(each):
        dispatch_copy(3, xi * each + q).start()
        for c in range(each + q * (m - 1), each + (q + 1) * (m - 1)):
            dispatch_copy(1, c).start()

    def small_copy(o, arriving=False):
        k = (ti + o) % nt
        return pltpu.make_async_remote_copy(
            src_ref=small_out.at[k], dst_ref=small_in.at[k if arriving else ti],
            send_sem=s_send.at[k], recv_sem=s_recv.at[k if arriving else ti],
            device_id={"task": k}, device_id_type=MESH)

    own = pick(zi)
    for c in range(chunks):
        held[zi, c] = gathered(own, c)

    def set_gate(d):
        hit = slot_across == column(row_of(place, d))
        gate[d] = jnp.where(hit, column(row_of(level_of, d)), 0.0).astype(BF16)

    w_load.wait()
    tw_load.wait()

    def rs_copy(s, o, l, arriving=False):
        j = (xi + o) % m
        return pltpu.make_async_remote_copy(
            src_ref=rs_out.at[s, j, l], dst_ref=rs_in.at[s, j if arriving else xi, l],
            send_sem=rs_send.at[s, j, l], recv_sem=rs_recv.at[s, j if arriving else xi, l],
            device_id={"mp": j}, device_id_type=MESH)

    def accumulate(sums, s, ats, fresh=False, finish=False):
        for c0 in range(0, units, step):
            acc = jnp.zeros((slots, step), F32) if fresh else sums[:, c0:c0 + step]
            for at in ats:
                acc += jnp.dot(
                    held[s, at], w[pl.ds(pl.multiple_of(at * depth, depth), depth), c0:c0 + step],
                    preferred_element_type=F32)
            if finish:
                hid[:, c0:c0 + step] = (acc * sigmoid(acc)).astype(BF16)
            else:
                sums[:, c0:c0 + step] = acc

    def own_chunk(q):
        return xi * each + q

    def other_chunks(q):
        return [(xi + o) % m * each + q for o in range(1, m)]

    def wait_others(s, q):
        for o in range(1, m):
            forward_copy(s, o, q, True).wait_recv()

    def tower_sums(s):
        for o in range(1, m):
            for l in range(tl):
                j = (xi + o) % m
                u = jnp.dot(hid[...], tw[j * tl + l], preferred_element_type=F32)
                rs_out[s, j, l] = u.astype(BF16)
                rs_copy(s, o, l).start()
        for l in range(tl):
            part[s, l] = jnp.dot(hid[...], tw[xi * tl + l], preferred_element_type=F32)

    def reduced(s, l):
        total = part[s, l]
        for o in range(1, m):
            rs_copy(s, o, l, True).wait_recv()
            total += rs_in[s, (xi + o) % m, l].astype(F32)
        return total.astype(BF16)

    def back_copy(s, l, arriving=False):
        return pltpu.make_async_remote_copy(
            src_ref=back_out.at[s, l], dst_ref=back_in.at[s if arriving else zi, l],
            send_sem=b_send.at[s, l], recv_sem=b_recv.at[s if arriving else zi, l],
            device_id={"dp": s}, device_id_type=MESH)

    def forward_copy(s, o, q, arriving=False):
        j = (xi + o) % m
        at = (j if arriving else xi) * each + q
        return pltpu.make_async_remote_copy(
            src_ref=held.at[s, at], dst_ref=held.at[s, at],
            send_sem=x_send.at[s, j, q], recv_sem=x_recv.at[s, at],
            device_id={"mp": j}, device_id_type=MESH)

    def forward(o, q):
        dispatch_copy(o, own_chunk(q), True).wait_recv()
        for p in range(1, m):
            forward_copy(partner(o), p, q).start()

    def send_back(s):
        for l in range(tl):
            back_out[s, l] = reduced(s, l)
            back_copy(s, l).start()

    accumulate(pre, zi, range(chunks), fresh=True, finish=True)
    forward(2, 0)
    tower_sums(zi)
    forward(2, 1)

    for copy in small_loads:
        copy.wait()
    for k in range(nt):
        small_out[k, 0:1, 0:rows] = cotangent[0:1, k * rows:(k + 1) * rows]
        small_out[k, 1:2, 0:ft] = tower_out[0:1, :]

    def send_small(o, c):
        small_copy(o).start()
        return c

    lax.fori_loop(1, nt, send_small, 0)
    small_in[ti] = small_out[ti]

    def work(o, c):
        s = partner(o)

        @pl.when(o + 2 < n)
        def _():
            for q in range(each):
                dispatch_copy(o, own_chunk(q)).wait_send()
                dispatch_copy(o + 2, own_chunk(q)).start()

        @pl.when(o > 2)
        def _():
            forward(o, 0)
            forward(o, 1)

        forward(o, 2)
        forward(o, 3)

        @pl.when(o > 2)
        def _():
            send_back(partner(o - 1))

        accumulate(pre, s, [own_chunk(q) for q in range(each)], fresh=True)
        set_gate(s)
        for q in range(each):
            wait_others(s, q)
        accumulate(
            pre, s, [at for q in range(each) for at in other_chunks(q)], finish=True)
        tower_sums(s)
        return c

    lax.fori_loop(2, n - 1, work, 0)

    near, last = partner(1), partner(n - 1)
    cuts = (0, chunks // 2, 3 * chunks // 4, chunks)

    def near_group(g):
        ats = range(cuts[g], cuts[g + 1])
        for at in ats:
            dispatch_copy(1, at, True).wait_recv()
        accumulate(near_pre, near, ats, fresh=g == 0, finish=g == 2)

    forward(n - 1, 0)
    forward(n - 1, 1)
    send_back(partner(n - 2))
    set_gate(last)
    near_group(0)
    forward(n - 1, 2)
    wait_others(last, 0)
    accumulate(pre, last, [own_chunk(0), own_chunk(1)] + other_chunks(0), fresh=True)
    near_group(1)
    forward(n - 1, 3)
    near_group(2)
    tower_sums(near)
    set_gate(near)
    wait_others(last, 1)
    wait_others(last, 2)
    accumulate(
        pre, last, [own_chunk(2), own_chunk(3)] + other_chunks(1) + other_chunks(2))
    send_back(near)
    set_gate(zi)
    scale = 1.0 / column(jnp.sum(level_of, axis=0, keepdims=True))
    zsum[...] = jnp.zeros_like(zsum)
    wait_others(last, 3)
    accumulate(pre, last, other_chunks(3), finish=True)
    tower_sums(last)
    send_back(last)
    for l in range(tl):
        zsum[l] += jnp.dot(gate[zi], reduced(zi, l), preferred_element_type=F32)

    def collect(s, l):
        back_copy(s, l, True).wait_recv()
        zsum[l] += jnp.dot(gate[s], back_in[s, l], preferred_element_type=F32)

    def collect_step(o, c):
        for l in range(tl):
            collect(partner(o), l)
        return c

    def small_arrive(o, c):
        small_copy(o, True).wait_recv()
        return c

    lax.fori_loop(1, nt, small_arrive, 0)
    cots = [column(small_in[xi * tl + l, 0:1, 0:rows]) for l in range(tl)]
    lax.fori_loop(2, n - 1, collect_step, 0)
    for l in range(tl):
        collect(near, l)

    def pred_copy(l, o):
        y = (xi + o) % m
        return pltpu.make_async_remote_copy(
            src_ref=pred_send.at[l], dst_ref=pred_in.at[ti], send_sem=p_send.at[l, o],
            recv_sem=p_recv.at[ti], device_id={"task": xi * tl + l, "mp": y},
            device_id_type=MESH)

    def dz_copy(l, o, arriving=False):
        j = (xi + o) % m
        at = (j if arriving else xi) * tl + l
        return pltpu.make_async_remote_copy(
            src_ref=dz.at[at], dst_ref=dz.at[at], send_sem=d_send.at[j, l],
            recv_sem=d_recv.at[at], device_id={"mp": j}, device_id_type=MESH)

    for l in range(tl):
        t = xi * tl + l
        collect(last, l)
        z = zsum[l] * scale
        s = sigmoid(z)
        out_row = small_in[t, 1:2, 0:ft]
        dz[t] = (cots[l] * out_row * s * (1.0 + z * (1.0 - s))).astype(BF16)
        for o in range(1, m):
            dz_copy(l, o).start()
        value = jnp.sum(z * s * out_row, axis=1, keepdims=True)
        pred_send[l, 0:1, 0:rows] = jnp.sum(jnp.where(diagonal, value, 0.0), axis=0, keepdims=True)
        mine = ti == t

        @pl.when(mine)
        def _():
            pred_in[ti] = pred_send[l]

        @pl.when(jnp.logical_not(mine))
        def _():
            pred_copy(l, 0).start()

        for o in range(1, m):
            pred_copy(l, o).start()

    def grad(o, c0):
        acc = jnp.zeros((rows, step), F32)
        for l in range(tl):
            t = (xi + o) % m * tl + l
            acc += lax.dot_general(
                dz[t], tw[t, c0:c0 + step, :], (((1,), (1,)), ((), ())),
                preferred_element_type=F32)
        return acc

    for c0 in range(0, units, step):
        gsum[:, c0:c0 + step] = grad(0, c0)
    for o in range(1, m):
        for l in range(tl):
            dz_copy(l, o, True).wait_recv()
    grad_writes = []
    for c0 in range(0, units, step):
        acc = gsum[:, c0:c0 + step]
        for o in range(1, m):
            acc += grad(o, c0)
        block = c0 // step
        gout[block] = acc.astype(BF16)
        grad_writes.append(pltpu.make_async_copy(
            gout.at[block], grad_out.at[:, pl.ds(c0, step)], out_sem.at[block]))
        grad_writes[-1].start()

    keeper = ti // tl
    for k in range(nt):
        @pl.when(jnp.logical_not(jnp.logical_and(keeper == xi, ti == k)))
        def _():
            pltpu.make_async_remote_copy(
                src_ref=pred_send.at[0], dst_ref=pred_in.at[k], send_sem=p_send.at[0, 0],
                recv_sem=p_recv.at[k], device_id={"task": (ti + 1) % nt},
                device_id_type=MESH).wait_recv()

        pred[0:1, k * rows:(k + 1) * rows] = pred_in[k, 0:1, 0:rows]

    pred_write = pltpu.make_async_copy(pred, pred_out, out_sem.at[units // step])
    pred_write.start()

    def drain(o, c):
        s = partner(o)
        for l in range(tl):
            back_copy(s, l).wait_send()
            for p in range(1, m):
                rs_copy(s, p, l).wait_send()
        return c

    def drain_far(o, c):
        for p in range(1, m):
            for q in range(each):
                forward_copy(partner(o), p, q).wait_send()
        return c

    lax.fori_loop(1, n, drain, 0)
    lax.fori_loop(2, n, drain_far, 0)
    for c in range(chunks):
        dispatch_copy(1, c).wait_send()
    for q in range(each):
        dispatch_copy(n - 2, xi * each + q).wait_send()
        dispatch_copy(n - 1, xi * each + q).wait_send()
    for p in range(1, m):
        for l in range(tl):
            rs_copy(zi, p, l).wait_send()
            dz_copy(l, p).wait_send()

    def drain_small(o, c):
        small_copy(o).wait_send()
        return c

    lax.fori_loop(1, nt, drain_small, 0)
    for l in range(tl):
        @pl.when(ti != xi * tl + l)
        def _():
            pred_copy(l, 0).wait_send()

        for o in range(1, m):
            pred_copy(l, o).wait_send()
    for copy in grad_writes:
        copy.wait()
    pred_write.wait()


def hand_over(pred, grad, pred_out, grad_out, pred_here, grad_here, sem):
    rows = grad.shape[0] // 4
    parts = [(pred, pred_here, pred_out)]
    for i in range(4):
        at = pl.ds(i * rows, rows)
        parts.append((grad.at[at, :], grad_here.at[at, :], grad_out.at[at, :]))
    reads = [pltpu.make_async_copy(a, b, sem.at[0, i]) for i, (a, b, _) in enumerate(parts)]
    writes = [pltpu.make_async_copy(b, c, sem.at[1, i]) for i, (_, b, c) in enumerate(parts)]
    for read in reads:
        read.start()
    for read, write in zip(reads, writes):
        read.wait()
        write.start()
    for write in writes:
        write.wait()


def body(tokens, expert_ids, gate_levels, expert_weight, tower_weight, tower_out, cotangent):
    n, nt, m = lax.axis_size("dp"), lax.axis_size("task"), lax.axis_size("mp")
    rows, top = expert_ids.shape
    width, units = expert_weight.shape[1:]
    ft = tower_weight.shape[2]
    slots = -(-(5 * rows * top // (4 * n)) // 16) * 16
    depth = width // m
    tl = nt // m
    step = 512 if units % 512 == 0 else units
    wide = -(-max(rows, ft) // 128) * 128
    each = 4
    chunks = m * each
    depth = width // chunks
    hbm = pl.BlockSpec(memory_space=pltpu.HBM)
    dma = pltpu.SemaphoreType.DMA
    pred, grad = pl.pallas_call(
        functools.partial(kernel, n, nt, m),
        out_shape=(
            jax.ShapeDtypeStruct((1, nt * rows), F32),
            jax.ShapeDtypeStruct((rows, units), BF16),
        ),
        in_specs=[hbm] * 7,
        out_specs=(hbm, hbm),
        scratch_shapes=[
            pltpu.VMEM((chunks, rows, depth), BF16),
            pltpu.VMEM((width, units), BF16),
            pltpu.VMEM(tower_weight.shape, BF16),
            pltpu.VMEM((top, rows), jnp.int32),
            pltpu.VMEM((top, rows), jnp.int32),
            pltpu.VMEM(tower_out.shape, F32),
            pltpu.VMEM(cotangent.shape, F32),
            pltpu.VMEM((n, chunks, slots, depth), BF16),
            pltpu.VMEM((n, chunks, slots, depth), BF16),
            pltpu.VMEM((n, rows, slots), BF16),
            pltpu.VMEM((slots, units), F32),
            pltpu.VMEM((slots, units), F32),
            pltpu.VMEM((slots, units), BF16),
            pltpu.VMEM((n, tl, slots, ft), F32),
            pltpu.VMEM((n, m, tl, slots, ft), BF16),
            pltpu.VMEM((n, m, tl, slots, ft), BF16),
            pltpu.VMEM((n, tl, slots, ft), BF16),
            pltpu.VMEM((n, tl, slots, ft), BF16),
            pltpu.VMEM((tl, rows, ft), F32),
            pltpu.VMEM((nt, rows, ft), BF16),
            pltpu.VMEM((rows, units), F32),
            pltpu.VMEM((units // step, rows, step), BF16),
            pltpu.VMEM((1, nt * rows), F32),
            pltpu.VMEM((nt, 8, wide), F32),
            pltpu.VMEM((nt, 8, wide), F32),
            pltpu.VMEM((tl, 8, wide), F32),
            pltpu.VMEM((nt, 8, wide), F32),
            dma((6 + chunks,)),
            dma((n, chunks)), dma((n, chunks)),
            dma((n, m, each)), dma((n, chunks)),
            dma((n, m, tl)), dma((n, m, tl)),
            dma((n, tl)), dma((n, tl)),
            dma((nt,)), dma((nt,)),
            dma((m, tl)), dma((nt,)),
            dma((tl, m)), dma((nt,)), dma((units // step + 1,)),
        ],
        compiler_params=pltpu.CompilerParams(
            collective_id=0, has_side_effects=True, vmem_limit_bytes=60 * 1024 * 1024),
        name="expert_towers",
    )(tokens, expert_ids.T, gate_levels.T, expert_weight, tower_weight, tower_out, cotangent)
    return tuple(pl.pallas_call(
        hand_over,
        out_shape=(
            jax.ShapeDtypeStruct(pred.shape, F32),
            jax.ShapeDtypeStruct(grad.shape, BF16),
        ),
        in_specs=[hbm] * 2,
        out_specs=(hbm, hbm),
        scratch_shapes=[
            pltpu.VMEM(pred.shape, F32), pltpu.VMEM(grad.shape, BF16), dma((2, 5))],
        compiler_params=pltpu.CompilerParams(vmem_limit_bytes=60 * 1024 * 1024),
        name="hand_over",
    )(pred, grad))


def solution(mesh):
    return jax.shard_map(
        body,
        mesh=mesh,
        in_specs=(
            P(("dp", "task"), None),
            P(("dp", "task"), None),
            P(("dp", "task"), None),
            P("dp", None, "mp"),
            P(None, "mp", None),
            P("task", None),
            P("task", "dp"),
        ),
        out_specs=(P("task", "dp"), P(("dp", "task"), "mp")),
        check_vma=False,
    )
```

```python
import functools

import jax
import jax.numpy as jnp
from jax import lax
from jax.experimental import pallas as pl
from jax.experimental.pallas import tpu as pltpu
from jax.sharding import PartitionSpec as P

MESH = pl.DeviceIdType.MESH
F32 = jnp.float32
BF16 = jnp.bfloat16


def sigmoid(v):
    return 0.5 + 0.5 * jnp.tanh(0.5 * v)


def kernel(
    n, nt, m,
    tokens, ids_in, levels_in, weight, towers, tower_out_in, cotangent_in,
    pred_out, grad_out,
    tok, w, tw, ids, levels, tower_out, cotangent,
    disp, held, gate, pre, near_pre, hid, part, rs_out, rs_in, back_out, back_in,
    zsum, dz, gsum, gout, pred, small_out, small_in, pred_send, pred_in,
    load_sem, z_send, z_recv, x_send, x_recv, rs_send, rs_recv, b_send, b_recv,
    s_send, s_recv, d_send, d_recv, p_send, p_recv, out_sem,
):
    zi, ti, xi = lax.axis_index("dp"), lax.axis_index("task"), lax.axis_index("mp")
    rows = ids.shape[1]
    slots = gate.shape[2]
    chunks, _, depth = tok.shape
    each = chunks // m
    units = w.shape[1]
    ft = towers.shape[2]
    tl = nt // m
    step = 512 if units % 512 == 0 else units

    def partner(o):
        other, bit = 0, 1
        while bit < n:
            other = other + bit * ((zi // bit + o // bit) % 2)
            bit *= 2
        return other

    def load(src, dst, i):
        copy = pltpu.make_async_copy(src, dst, load_sem.at[i])
        copy.start()
        return copy

    routing = [load(ids_in, ids, 0), load(levels_in, levels, 1)]
    tok_loads = [
        load(tokens.at[:, pl.ds(c * depth, depth)], tok.at[c], 6 + c) for c in range(chunks)]
    small_loads = [load(tower_out_in, tower_out, 2), load(cotangent_in, cotangent, 3)]

    barrier = pltpu.get_barrier_semaphore()

    def greet_line(o, c):
        pl.semaphore_signal(barrier, inc=1, device_id={"dp": partner(o)}, device_id_type=MESH)
        return c

    def greet_plane(o, c):
        at = (ti * m + xi + o) % (nt * m)
        pl.semaphore_signal(
            barrier, inc=1, device_id={"task": at // m, "mp": at % m}, device_id_type=MESH)
        return c

    lax.fori_loop(1, n, greet_line, 0)
    lax.fori_loop(1, nt * m, greet_plane, 0)

    for copy in routing:
        copy.wait()
    names = max(8, n)
    sub = lax.broadcasted_iota(jnp.int32, (names, rows), 0)
    level_of = (
        jnp.where(ids[0:1, :] == sub, levels[0:1, :], 0)
        + jnp.where(ids[1:2, :] == sub, levels[1:2, :], 0)).astype(F32)
    named = jnp.where(level_of > 0, 1.0, 0.0)
    down = lax.broadcasted_iota(jnp.int32, (rows, rows), 0)
    across = lax.broadcasted_iota(jnp.int32, (rows, rows), 1)
    diagonal = down == across
    before = jnp.where(down < across, 1.0, 0.0)
    rank = jnp.dot(named.astype(BF16), before.astype(BF16), preferred_element_type=F32)
    place = jnp.where(named > 0, rank, -1.0)

    def row_of(table, d):
        return jnp.sum(jnp.where(sub == d, table, 0.0), axis=0, keepdims=True)

    def column(row):
        return jnp.sum(jnp.where(diagonal, row, 0.0), axis=1, keepdims=True)

    slot_down = lax.broadcasted_iota(jnp.int32, (slots, rows), 0).astype(F32)
    slot_across = lax.broadcasted_iota(jnp.int32, (rows, slots), 1).astype(F32)

    def pick(d):
        return jnp.where(slot_down == row_of(place, d), 1.0, 0.0).astype(BF16)

    def gathered(spot, c):
        return jnp.dot(spot, tok[c], preferred_element_type=F32).astype(BF16)

    for copy in tok_loads:
        copy.wait()
    w_load = load(weight.at[0], w, 4)
    tw_load = load(towers, tw, 5)

    def dispatch_copy(o, c, arriving=False):
        d = partner(o)
        return pltpu.make_async_remote_copy(
            src_ref=disp.at[d, c], dst_ref=held.at[d if arriving else zi, c],
            send_sem=z_send.at[d, c], recv_sem=z_recv.at[d if arriving else zi, c],
            device_id={"dp": d}, device_id_type=MESH)

    def fill(o, first, count):
        d = partner(o)
        spot = pick(d)
        for q in range(count):
            disp[d, first + q] = gathered(spot, first + q)

    fill(2, xi * each, each)
    pl.semaphore_wait(barrier, n - 1 + nt * m - 1)
    dispatch_copy(2, xi * each).start()
    fill(1, 0, chunks)
    for q in range(each):
        if q > 0:
            dispatch_copy(2, xi * each + q).start()
        dispatch_copy(1, q).start()

    def fill_rest(o, c):
        fill(o, xi * each, each)
        return c

    lax.fori_loop(3, n, fill_rest, 0)
    for q in range(each):
        dispatch_copy(3, xi * each + q).start()
        for c in range(each + q * (m - 1), each + (q + 1) * (m - 1)):
            dispatch_copy(1, c).start()

    def small_copy(o, arriving=False):
        k = (ti + o) % nt
        return pltpu.make_async_remote_copy(
            src_ref=small_out.at[k], dst_ref=small_in.at[k if arriving else ti],
            send_sem=s_send.at[k], recv_sem=s_recv.at[k if arriving else ti],
            device_id={"task": k}, device_id_type=MESH)

    own = pick(zi)
    for c in range(chunks):
        held[zi, c] = gathered(own, c)

    def set_gate(d):
        hit = slot_across == column(row_of(place, d))
        gate[d] = jnp.where(hit, column(row_of(level_of, d)), 0.0).astype(BF16)

    w_load.wait()
    tw_load.wait()

    def rs_copy(s, o, l, arriving=False):
        j = (xi + o) % m
        return pltpu.make_async_remote_copy(
            src_ref=rs_out.at[s, j, l], dst_ref=rs_in.at[s, j if arriving else xi, l],
            send_sem=rs_send.at[s, j, l], recv_sem=rs_recv.at[s, j if arriving else xi, l],
            device_id={"mp": j}, device_id_type=MESH)

    def accumulate(sums, s, ats, fresh=False, finish=False):
        for c0 in range(0, units, step):
            acc = jnp.zeros((slots, step), F32) if fresh else sums[:, c0:c0 + step]
            for at in ats:
                acc += jnp.dot(
                    held[s, at], w[pl.ds(pl.multiple_of(at * depth, depth), depth), c0:c0 + step],
                    preferred_element_type=F32)
            if finish:
                hid[:, c0:c0 + step] = (acc * sigmoid(acc)).astype(BF16)
            else:
                sums[:, c0:c0 + step] = acc

    def own_chunk(q):
        return xi * each + q

    def other_chunks(q):
        return [(xi + o) % m * each + q for o in range(1, m)]

    def wait_others(s, q):
        for o in range(1, m):
            forward_copy(s, o, q, True).wait_recv()

    def tower_sums(s):
        for o in range(1, m):
            for l in range(tl):
                j = (xi + o) % m
                u = jnp.dot(hid[...], tw[j * tl + l], preferred_element_type=F32)
                rs_out[s, j, l] = u.astype(BF16)
                rs_copy(s, o, l).start()
        for l in range(tl):
            part[s, l] = jnp.dot(hid[...], tw[xi * tl + l], preferred_element_type=F32)

    def reduced(s, l):
        total = part[s, l]
        for o in range(1, m):
            rs_copy(s, o, l, True).wait_recv()
            total += rs_in[s, (xi + o) % m, l].astype(F32)
        return total.astype(BF16)

    def back_copy(s, l, arriving=False):
        return pltpu.make_async_remote_copy(
            src_ref=back_out.at[s, l], dst_ref=back_in.at[s if arriving else zi, l],
            send_sem=b_send.at[s, l], recv_sem=b_recv.at[s if arriving else zi, l],
            device_id={"dp": s}, device_id_type=MESH)

    def forward_copy(s, o, q, arriving=False):
        j = (xi + o) % m
        at = (j if arriving else xi) * each + q
        return pltpu.make_async_remote_copy(
            src_ref=held.at[s, at], dst_ref=held.at[s, at],
            send_sem=x_send.at[s, j, q], recv_sem=x_recv.at[s, at],
            device_id={"mp": j}, device_id_type=MESH)

    def forward(o, q):
        dispatch_copy(o, own_chunk(q), True).wait_recv()
        for p in range(1, m):
            forward_copy(partner(o), p, q).start()

    def send_back(s):
        for l in range(tl):
            back_out[s, l] = reduced(s, l)
            back_copy(s, l).start()

    accumulate(pre, zi, range(chunks), fresh=True, finish=True)
    forward(2, 0)
    tower_sums(zi)
    forward(2, 1)

    for copy in small_loads:
        copy.wait()
    for k in range(nt):
        small_out[k, 0:1, 0:rows] = cotangent[0:1, k * rows:(k + 1) * rows]
        small_out[k, 1:2, 0:ft] = tower_out[0:1, :]

    def send_small(o, c):
        small_copy(o).start()
        return c

    lax.fori_loop(1, nt, send_small, 0)
    small_in[ti] = small_out[ti]

    def work(o, c):
        s = partner(o)

        @pl.when(o + 2 < n)
        def _():
            for q in range(each):
                dispatch_copy(o, own_chunk(q)).wait_send()
                dispatch_copy(o + 2, own_chunk(q)).start()

        @pl.when(o > 2)
        def _():
            forward(o, 0)
            forward(o, 1)

        forward(o, 2)
        forward(o, 3)

        @pl.when(o > 2)
        def _():
            send_back(partner(o - 1))

        accumulate(pre, s, [own_chunk(q) for q in range(each)], fresh=True)
        set_gate(s)
        for q in range(each):
            wait_others(s, q)
        accumulate(
            pre, s, [at for q in range(each) for at in other_chunks(q)], finish=True)
        tower_sums(s)
        return c

    lax.fori_loop(2, n - 1, work, 0)

    near, last = partner(1), partner(n - 1)
    cuts = (0, chunks // 2, 3 * chunks // 4, chunks)

    def near_group(g):
        ats = range(cuts[g], cuts[g + 1])
        for at in ats:
            dispatch_copy(1, at, True).wait_recv()
        accumulate(near_pre, near, ats, fresh=g == 0, finish=g == 2)

    forward(n - 1, 0)
    forward(n - 1, 1)
    send_back(partner(n - 2))
    set_gate(last)
    near_group(0)
    forward(n - 1, 2)
    wait_others(last, 0)
    accumulate(pre, last, [own_chunk(0), own_chunk(1)] + other_chunks(0), fresh=True)
    near_group(1)
    forward(n - 1, 3)
    near_group(2)
    tower_sums(near)
    set_gate(near)
    wait_others(last, 1)
    wait_others(last, 2)
    accumulate(
        pre, last, [own_chunk(2), own_chunk(3)] + other_chunks(1) + other_chunks(2))
    send_back(near)
    set_gate(zi)
    scale = 1.0 / column(jnp.sum(level_of, axis=0, keepdims=True))
    zsum[...] = jnp.zeros_like(zsum)
    wait_others(last, 3)
    accumulate(pre, last, other_chunks(3), finish=True)
    tower_sums(last)
    send_back(last)
    for l in range(tl):
        zsum[l] += jnp.dot(gate[zi], reduced(zi, l), preferred_element_type=F32)

    def collect(s, l):
        back_copy(s, l, True).wait_recv()
        zsum[l] += jnp.dot(gate[s], back_in[s, l], preferred_element_type=F32)

    def collect_step(o, c):
        for l in range(tl):
            collect(partner(o), l)
        return c

    def small_arrive(o, c):
        small_copy(o, True).wait_recv()
        return c

    lax.fori_loop(1, nt, small_arrive, 0)
    cots = [column(small_in[xi * tl + l, 0:1, 0:rows]) for l in range(tl)]
    lax.fori_loop(2, n - 1, collect_step, 0)
    for l in range(tl):
        collect(near, l)

    def pred_copy(l, o):
        y = (xi + o) % m
        return pltpu.make_async_remote_copy(
            src_ref=pred_send.at[l], dst_ref=pred_in.at[ti], send_sem=p_send.at[l, o],
            recv_sem=p_recv.at[ti], device_id={"task": xi * tl + l, "mp": y},
            device_id_type=MESH)

    def dz_copy(l, o, arriving=False):
        j = (xi + o) % m
        at = (j if arriving else xi) * tl + l
        return pltpu.make_async_remote_copy(
            src_ref=dz.at[at], dst_ref=dz.at[at], send_sem=d_send.at[j, l],
            recv_sem=d_recv.at[at], device_id={"mp": j}, device_id_type=MESH)

    for l in range(tl):
        t = xi * tl + l
        collect(last, l)
        z = zsum[l] * scale
        s = sigmoid(z)
        out_row = small_in[t, 1:2, 0:ft]
        dz[t] = (cots[l] * out_row * s * (1.0 + z * (1.0 - s))).astype(BF16)
        for o in range(1, m):
            dz_copy(l, o).start()
        value = jnp.sum(z * s * out_row, axis=1, keepdims=True)
        pred_send[l, 0:1, 0:rows] = jnp.sum(jnp.where(diagonal, value, 0.0), axis=0, keepdims=True)
        mine = ti == t

        @pl.when(mine)
        def _():
            pred_in[ti] = pred_send[l]

        @pl.when(jnp.logical_not(mine))
        def _():
            pred_copy(l, 0).start()

        for o in range(1, m):
            pred_copy(l, o).start()

    def grad(o, c0):
        acc = jnp.zeros((rows, step), F32)
        for l in range(tl):
            t = (xi + o) % m * tl + l
            acc += lax.dot_general(
                dz[t], tw[t, c0:c0 + step, :], (((1,), (1,)), ((), ())),
                preferred_element_type=F32)
        return acc

    for c0 in range(0, units, step):
        gsum[:, c0:c0 + step] = grad(0, c0)
    for o in range(1, m):
        for l in range(tl):
            dz_copy(l, o, True).wait_recv()
    grad_writes = []
    for c0 in range(0, units, step):
        acc = gsum[:, c0:c0 + step]
        for o in range(1, m):
            acc += grad(o, c0)
        block = c0 // step
        gout[block] = acc.astype(BF16)
        grad_writes.append(pltpu.make_async_copy(
            gout.at[block], grad_out.at[:, pl.ds(c0, step)], out_sem.at[block]))
        grad_writes[-1].start()

    keeper = ti // tl
    for k in range(nt):
        @pl.when(jnp.logical_not(jnp.logical_and(keeper == xi, ti == k)))
        def _():
            pltpu.make_async_remote_copy(
                src_ref=pred_send.at[0], dst_ref=pred_in.at[k], send_sem=p_send.at[0, 0],
                recv_sem=p_recv.at[k], device_id={"task": (ti + 1) % nt},
                device_id_type=MESH).wait_recv()

        pred[0:1, k * rows:(k + 1) * rows] = pred_in[k, 0:1, 0:rows]

    pred_write = pltpu.make_async_copy(pred, pred_out, out_sem.at[units // step])
    pred_write.start()

    def drain(o, c):
        s = partner(o)
        for l in range(tl):
            back_copy(s, l).wait_send()
            for p in range(1, m):
                rs_copy(s, p, l).wait_send()
        return c

    def drain_far(o, c):
        for p in range(1, m):
            for q in range(each):
                forward_copy(partner(o), p, q).wait_send()
        return c

    lax.fori_loop(1, n, drain, 0)
    lax.fori_loop(2, n, drain_far, 0)
    for c in range(chunks):
        dispatch_copy(1, c).wait_send()
    for q in range(each):
        dispatch_copy(n - 2, xi * each + q).wait_send()
        dispatch_copy(n - 1, xi * each + q).wait_send()
    for p in range(1, m):
        for l in range(tl):
            rs_copy(zi, p, l).wait_send()
            dz_copy(l, p).wait_send()

    def drain_small(o, c):
        small_copy(o).wait_send()
        return c

    lax.fori_loop(1, nt, drain_small, 0)
    for l in range(tl):
        @pl.when(ti != xi * tl + l)
        def _():
            pred_copy(l, 0).wait_send()

        for o in range(1, m):
            pred_copy(l, o).wait_send()
    for copy in grad_writes:
        copy.wait()
    pred_write.wait()


def hand_over(pred, grad, pred_out, grad_out, pred_here, grad_here, sem):
    rows = grad.shape[0] // 4
    parts = [(pred, pred_here, pred_out)]
    for i in range(4):
        at = pl.ds(i * rows, rows)
        parts.append((grad.at[at, :], grad_here.at[at, :], grad_out.at[at, :]))
    reads = [pltpu.make_async_copy(a, b, sem.at[0, i]) for i, (a, b, _) in enumerate(parts)]
    writes = [pltpu.make_async_copy(b, c, sem.at[1, i]) for i, (_, b, c) in enumerate(parts)]
    for read in reads:
        read.start()
    for read, write in zip(reads, writes):
        read.wait()
        write.start()
    for write in writes:
        write.wait()


def body(tokens, expert_ids, gate_levels, expert_weight, tower_weight, tower_out, cotangent):
    n, nt, m = lax.axis_size("dp"), lax.axis_size("task"), lax.axis_size("mp")
    rows, top = expert_ids.shape
    width, units = expert_weight.shape[1:]
    ft = tower_weight.shape[2]
    slots = -(-(5 * rows * top // (4 * n)) // 16) * 16
    depth = width // m
    tl = nt // m
    step = 512 if units % 512 == 0 else units
    wide = -(-max(rows, ft) // 128) * 128
    each = 4
    chunks = m * each
    depth = width // chunks
    hbm = pl.BlockSpec(memory_space=pltpu.HBM)
    dma = pltpu.SemaphoreType.DMA
    pred, grad = pl.pallas_call(
        functools.partial(kernel, n, nt, m),
        out_shape=(
            jax.ShapeDtypeStruct((1, nt * rows), F32),
            jax.ShapeDtypeStruct((rows, units), BF16),
        ),
        in_specs=[hbm] * 7,
        out_specs=(hbm, hbm),
        scratch_shapes=[
            pltpu.VMEM((chunks, rows, depth), BF16),
            pltpu.VMEM((width, units), BF16),
            pltpu.VMEM(tower_weight.shape, BF16),
            pltpu.VMEM((top, rows), jnp.int32),
            pltpu.VMEM((top, rows), jnp.int32),
            pltpu.VMEM(tower_out.shape, F32),
            pltpu.VMEM(cotangent.shape, F32),
            pltpu.VMEM((n, chunks, slots, depth), BF16),
            pltpu.VMEM((n, chunks, slots, depth), BF16),
            pltpu.VMEM((n, rows, slots), BF16),
            pltpu.VMEM((slots, units), F32),
            pltpu.VMEM((slots, units), F32),
            pltpu.VMEM((slots, units), BF16),
            pltpu.VMEM((n, tl, slots, ft), F32),
            pltpu.VMEM((n, m, tl, slots, ft), BF16),
            pltpu.VMEM((n, m, tl, slots, ft), BF16),
            pltpu.VMEM((n, tl, slots, ft), BF16),
            pltpu.VMEM((n, tl, slots, ft), BF16),
            pltpu.VMEM((tl, rows, ft), F32),
            pltpu.VMEM((nt, rows, ft), BF16),
            pltpu.VMEM((rows, units), F32),
            pltpu.VMEM((units // step, rows, step), BF16),
            pltpu.VMEM((1, nt * rows), F32),
            pltpu.VMEM((nt, 8, wide), F32),
            pltpu.VMEM((nt, 8, wide), F32),
            pltpu.VMEM((tl, 8, wide), F32),
            pltpu.VMEM((nt, 8, wide), F32),
            dma((6 + chunks,)),
            dma((n, chunks)), dma((n, chunks)),
            dma((n, m, each)), dma((n, chunks)),
            dma((n, m, tl)), dma((n, m, tl)),
            dma((n, tl)), dma((n, tl)),
            dma((nt,)), dma((nt,)),
            dma((m, tl)), dma((nt,)),
            dma((tl, m)), dma((nt,)), dma((units // step + 1,)),
        ],
        compiler_params=pltpu.CompilerParams(
            collective_id=0, has_side_effects=True, vmem_limit_bytes=60 * 1024 * 1024),
        name="expert_towers",
    )(tokens, expert_ids.T, gate_levels.T, expert_weight, tower_weight, tower_out, cotangent)
    return tuple(pl.pallas_call(
        hand_over,
        out_shape=(
            jax.ShapeDtypeStruct(pred.shape, F32),
            jax.ShapeDtypeStruct(grad.shape, BF16),
        ),
        in_specs=[hbm] * 2,
        out_specs=(hbm, hbm),
        scratch_shapes=[
            pltpu.VMEM(pred.shape, F32), pltpu.VMEM(grad.shape, BF16), dma((2, 5))],
        compiler_params=pltpu.CompilerParams(vmem_limit_bytes=60 * 1024 * 1024),
        name="hand_over",
    )(pred, grad))


def solution(mesh):
    return jax.shard_map(
        body,
        mesh=mesh,
        in_specs=(
            P(("dp", "task"), None),
            P(("dp", "task"), None),
            P(("dp", "task"), None),
            P("dp", None, "mp"),
            P(None, "mp", None),
            P("task", None),
            P("task", "dp"),
        ),
        out_specs=(P("task", "dp"), P(("dp", "task"), "mp")),
        check_vma=False,
    )
```
